32 devices in a mesh: leaf: 32 (over z, y, x, core).
Axes of the slice: x: 2, y: 2, z: 4, core: 2. Of those that a mesh axis runs over, the one named last changes fastest.
Arguments:
- coords: float32 [3, 16384], P(None, 'leaf'), may hold values from 0 to 32, as said below
- weights: float32 [16384, 256], P('leaf'), may hold values from -6 to 6
- near_mask: int32 [32, 4], P('leaf'), may hold values 0 or 1
- leaf_inverse: float32 [16384, 512], P('leaf'), may hold values from -0.25 to 0.25
- up_basis: float32 [4, 16384, 512], P(None, 'leaf'), may hold values from -0.25 to 0.25
- coupling: float32 [4, 16384, 1024], P(None, 'leaf'), may hold values from -0.1875 to 0.1875
- down_basis: float32 [4, 16384, 512], P(None, 'leaf'), may hold values from -0.125 to 0.125
Outputs:
- solution: float32 [16384, 256], P('leaf')
The draws below stay inside these ranges and needn't reach their ends.
Inputs may be any that keep to these rules, and one draw needn't show every extreme that they name: The points of leaf i have i * 512 / 1024 <= coords[0] <= (i + 1) * 512 / 1024; their other two coordinates lie in [0, 32).
All inputs are finite; a program needn't handle non-finite values. No bound on the sum of `near_mask` on one device may be relied on, other than what follows from the above.
Results may differ from the reference program's by a relative error of at most 0.0003.
Values sent between devices are 32-bit elements; how exact they have to be, the bound alone decides.
No kernel may reach another device: no remote copies, remote signals or barrier semaphores. Data moves between devices by JAX's collectives and lax.ppermute only.
A program may use at most 64 MiB of HBM per device.

```python
import math
import jax
import jax.numpy as jnp
from jax import lax

LEAF = 512
RHS = 256
RANK = 512
LEVELS = 4
LEAVES = 32
POINTS = 16384
N_LEAF = 32


def draw_coords(key, part):
    key = jax.random.fold_in(key, 17)
    subkeys = jax.random.split(key, 3)
    across = jax.random.uniform(subkeys[0], (POINTS,), jnp.float32)
    lateral = jax.random.uniform(subkeys[1], (POINTS,), jnp.float32)
    vertical = jax.random.uniform(subkeys[2], (POINTS,), jnp.float32)
    slab_index = (jnp.arange(POINTS, dtype=jnp.int32) // LEAF).astype(jnp.float32)
    forward = (slab_index + across) * (LEAF / 1024.0)
    return jnp.stack([forward, 32.0 * lateral, 32.0 * vertical]).astype(jnp.float32)


def set_ends(values, key, least, high):
    extent = values.shape
    index_at = [jax.random.randint(jax.random.fold_in(key, axis), (), 0, extent[axis]) for axis in range(len(extent))]
    values = values.at[tuple(index_at)].set(least)
    longest = extent.index(max(extent))
    index_at[longest] = (index_at[longest] + 1) % extent[longest]
    return values.at[tuple(index_at)].set(high)


def block_levels(key, shape, cuts, low, high):
    level, own = 1.0, jax.random.fold_in(key, 6)
    for axis_at, shards_of in cuts:
        heights = jnp.exp(jax.random.uniform(jax.random.fold_in(own, axis_at), (shards_of,), jnp.float32, low / len(cuts), high / len(cuts)))
        level = level * jnp.repeat(heights, shape[axis_at] // shards_of).reshape([-1 if axis == axis_at else 1 for axis in range(len(shape))])
    return level


def noise(own_key, extent, scale, bound, cuts=(), kind=jnp.bfloat16):
    level = block_levels(own_key, extent, cuts, -0.22, 0.18) if cuts else 1.0
    result = jax.random.normal(own_key, extent, jnp.float32) * scale * level
    return jnp.minimum(jnp.maximum(result, -bound), bound).astype(kind)


def setup_inputs(seed: int = 0) -> dict:
    arg_keys = jax.random.split(jax.random.key(seed), 8)
    return {
        "coords": draw_coords(jax.random.fold_in(arg_keys[7], 71), 0),
        "weights": noise(arg_keys[1], (POINTS, RHS), 1.0, 6.0, ((0, 32),), jnp.float32),
        "near_mask": set_ends((jax.random.randint(arg_keys[2], (LEAVES, 4), 0, 3) < 2).astype(jnp.int32), jax.random.fold_in(arg_keys[2], 1), 0, 1),
        "leaf_inverse": noise(arg_keys[3], (POINTS, LEAF), LEAF ** -0.5, 0.25, ((0, 32),), jnp.float32),
        "up_basis": noise(arg_keys[4], (LEVELS, POINTS, RANK), LEAF ** -0.5, 0.25, ((1, 32),), jnp.float32),
        "coupling": noise(arg_keys[5], (LEVELS, LEAVES * RANK, 2 * RANK), (2 * RANK) ** -0.5, 0.1875, ((1, 32),), jnp.float32),
        "down_basis": noise(arg_keys[6], (LEVELS, POINTS, RANK), (4 * RANK) ** -0.5, 0.125, ((1, 32),), jnp.float32),
    }


OFFSETS = (-2, -1, 1, 2)

def batch_gauss(left, right):
    dist = jnp.zeros((left.shape[0], left.shape[2], right.shape[2]), jnp.float32)
    for coord in range(3):
        diff = left[:, coord, :, None] - right[:, coord, None, :]
        dist = dist + diff * diff
    return jnp.exp(-0.5 * dist)

def batch_tile(left, right, values):
    return jnp.einsum('lpq,lqc->lpc', batch_gauss(left, right), values, precision=lax.Precision.HIGHEST)

def reference(coords, weights, near_mask, leaf_inverse, up_basis, coupling, down_basis):
    count = N_LEAF
    points = coords.reshape(3, count, LEAF).transpose(1, 0, 2)
    values = weights.reshape(count, LEAF, RHS)
    pad_points = jnp.pad(points, ((2, 2), (0, 0), (0, 0)))
    pad_values = jnp.pad(values, ((2, 2), (0, 0), (0, 0)))
    total = batch_tile(points, points, values)
    for slot, offset in enumerate(OFFSETS):
        other_points = pad_points[2 + offset:2 + offset + count]
        other_values = pad_values[2 + offset:2 + offset + count]
        flags = near_mask[:, slot].astype(jnp.float32)[:, None, None]
        total = total + flags * batch_tile(points, other_points, other_values)
    near = total * 0.5
    iterate = jnp.einsum('lpq,lqc->lpc', leaf_inverse.reshape(count, LEAF, LEAF), near, precision=lax.Precision.HIGHEST)
    for level in range(LEVELS):
        width = 2 ** level
        skeleton = jnp.einsum('lpr,lpc->lrc', up_basis[level].reshape(count, LEAF, RANK), iterate, precision=lax.Precision.HIGHEST)
        grouped = skeleton.reshape(count // width, width, RANK, RHS).sum(axis=1, keepdims=True)
        grouped = jnp.broadcast_to(grouped, (count // width, width, RANK, RHS)).reshape(count, RANK, RHS)
        partner = grouped.reshape(count // (2 * width), 2, width, RANK, RHS)[:, ::-1].reshape(count, RANK, RHS)
        stacked = jnp.concatenate([grouped, partner], axis=1)
        factor = coupling[level].reshape(count, RANK, 2 * RANK)
        correction = jnp.einsum('lrs,lsc->lrc', factor, stacked, precision=lax.Precision.HIGHEST) * (1.0 / math.sqrt(2.0 ** (level + 1)))
        iterate = iterate - jnp.einsum('lpr,lrc->lpc', down_basis[level].reshape(count, LEAF, RANK), correction, precision=lax.Precision.HIGHEST)
    return iterate.reshape(count * LEAF, RHS)
```

```python
import math

import jax
import jax.numpy as jnp
from jax import lax
from jax.sharding import PartitionSpec as P

LEVELS = 4
CHUNKS = 2


def exchange(x, bit):
    count = lax.axis_size("leaf")
    return lax.ppermute(x, "leaf", [(i, i ^ bit) for i in range(count)])


def relay(x):
    count = lax.axis_size("leaf")
    return lax.ppermute(
        x, "leaf", [(i, (i + (-4 if i & 2 else 4)) % count) for i in range(count)]
    )


def product(left, right, contract=1):
    return lax.dot_general(
        left,
        right,
        (((contract,), (0,)), ((), ())),
        precision=lax.Precision.HIGH,
        preferred_element_type=jnp.float32,
    )


def tile(own, message, flag, rows):
    dist = jnp.zeros((own.shape[0], rows), jnp.float32)
    for coord in range(3):
        diff = own[:, coord][:, None] - message[rows + coord][None, :]
        dist = dist + diff * diff
    return flag * product(jnp.exp(-0.5 * dist), message[:rows])


def near_field(coords, weights, near_mask):
    me, count = lax.axis_index("leaf"), lax.axis_size("leaf")
    core, upper = me & 1, (me >> 1) & 1
    rows = weights.shape[0] // CHUNKS
    own = coords.T

    def flag(offset):
        slot = jnp.where(offset < 0, offset + 2, offset + 1)
        inside = (me + offset >= 0) & (me + offset < count)
        return jnp.where(inside, near_mask[0, slot], 0).astype(jnp.float32)

    one, two = 1 - 2 * core, 2 - 4 * upper
    messages = [
        jnp.concatenate(
            [
                weights[k * rows : (k + 1) * rows],
                coords[:, k * rows : (k + 1) * rows],
                jnp.zeros((5, rows), jnp.float32),
            ]
        )
        for k in range(CHUNKS)
    ]
    across = [exchange(m, 2) for m in messages]
    beside = [exchange(m, 1) for m in messages]
    passed = [relay(m) for m in across]
    crossed = [exchange(jnp.where(upper == core, a, p), 1) for a, p in zip(across, passed)]
    total = 0.0
    for m in messages:
        total = total + tile(own, m, 1.0, rows)
    for parts, offset in ((beside, one), (across, two), (passed, -two), (crossed, -one)):
        for m in parts:
            total = total + tile(own, m, flag(offset), rows)
    return total * 0.5


def level_step(iterate, level, up_basis, coupling, down_basis):
    core = lax.axis_index("leaf") & 1
    skeleton = product(up_basis[level], iterate, 0)
    half = skeleton.shape[0] // 2
    low, high = skeleton[:half], skeleton[half:]
    if level == 0:
        block, partner = skeleton, exchange(skeleton, 1)
    else:
        mine = jnp.where(core == 0, low, high) + exchange(jnp.where(core == 0, high, low), 1)
        for lower in range(1, level):
            mine = mine + exchange(mine, 1 << lower)
        theirs = exchange(mine, 1 << level)

        def whole(part):
            other = exchange(part, 1)
            return jnp.where(
                core == 0, jnp.concatenate([part, other]), jnp.concatenate([other, part])
            )

        block, partner = whole(mine), whole(theirs)
    rank = skeleton.shape[0]
    factor = coupling[level]
    correction = (product(factor[:, :rank], block) + product(factor[:, rank:], partner)) * (
        1.0 / math.sqrt(2.0 ** (level + 1))
    )
    return iterate - product(down_basis[level], correction)


def per_device(coords, weights, near_mask, leaf_inverse, up_basis, coupling, down_basis):
    near = near_field(coords, weights, near_mask)
    iterate = product(leaf_inverse, near)
    for level in range(LEVELS):
        iterate = level_step(iterate, level, up_basis, coupling, down_basis)
    return iterate


def solution(mesh):
    in_specs = (
        P(None, "leaf"),
        P("leaf", None),
        P("leaf", None),
        P("leaf", None),
        P(None, "leaf", None),
        P(None, "leaf", None),
        P(None, "leaf", None),
    )
    return jax.shard_map(
        per_device, mesh=mesh, in_specs=in_specs, out_specs=P("leaf", None), check_vma=False
    )
```

```python
import functools
import math
from typing import Any, NamedTuple

import jax
import jax.numpy as jnp
from jax import lax
from jax.experimental import pallas as pl
from jax.experimental.pallas import tpu as pltpu
from jax.sharding import PartitionSpec as P

LEVELS = 4
CHUNKS = 2
PAD = 8
F32, BF16 = jnp.float32, jnp.bfloat16
VMEM, WINDOW_VMEM = 24 * 2**20, 48 * 2**20
ALL = slice(None)


def permute(x, target):
    count = lax.axis_size("leaf")
    return lax.ppermute(x, "leaf", [(i, target(i) % count) for i in range(count)])


def exchange(x, bit):
    return permute(x, lambda i: i ^ bit)


def after(x, *earlier):
    return lax.optimization_barrier((x, *earlier))[0]


def split(x):
    high = x.astype(BF16)
    return high, (x - high.astype(F32)).astype(BF16)


def product(left, right):
    def dot(a, b):
        return jnp.dot(a, b, preferred_element_type=F32)

    (left_high, left_low), (right_high, right_low) = left, right
    rows, columns = left_high.shape[0], right_high.shape[1]
    count = 2 if columns <= 256 else 1
    got = []
    for k in range(count):
        at = slice(k * rows // count, (k + 1) * rows // count)
        high, low = left_high[at], left_low[at]
        got.append(dot(high, right_high) + (dot(high, right_low) + dot(low, right_high)))
    return jnp.concatenate(got) if count > 1 else got[0]


def parts(refs, index=...):
    return tuple(ref[index] for ref in refs)


def put(refs, index, values):
    for ref, value in zip(refs, values):
        ref[index] = value


def two_parts(*shape):
    return [(shape, BF16)] * 2


class Window(NamedTuple):
    array: Any
    index: tuple
    shape: tuple


class Arriving:
    def __init__(self, copy, ref):
        self.copy, self.ref, self.here = copy, ref, False

    def __call__(self):
        if not self.here:
            self.copy.wait()
            self.here = True
        return self.ref[...]


def call(body, outs, *args):
    windows = [arg for arg in args if isinstance(arg, Window)]
    arrays = [arg.array if isinstance(arg, Window) else arg for arg in args]

    def kernel(*refs):
        ins, rest = list(refs[: len(args)]), refs[len(args) :]
        results, buffers, semaphores = rest[: len(outs)], rest[len(outs) : -1], rest[-1]
        arriving = []
        for k, arg in enumerate(args):
            if isinstance(arg, Window):
                at = len(arriving)
                copy = pltpu.make_async_copy(ins[k].at[arg.index], buffers[at], semaphores.at[at])
                copy.start()
                ins[k] = Arriving(copy, buffers[at])
                arriving.append(ins[k])
        body(*ins, *results)
        for window in arriving:
            if not window.here:
                window.copy.wait()

    def spec(arg):
        if isinstance(arg, Window):
            return pl.BlockSpec(memory_space=pltpu.HBM)
        return pl.BlockSpec(memory_space=pltpu.SMEM if arg.dtype == jnp.int32 else pltpu.VMEM)

    return pl.pallas_call(
        kernel,
        in_specs=[spec(arg) for arg in args],
        out_specs=[pl.BlockSpec(memory_space=pltpu.VMEM) for _ in outs],
        out_shape=[jax.ShapeDtypeStruct(*out) for out in outs],
        scratch_shapes=[pltpu.VMEM(w.shape, w.array.dtype) for w in windows]
        + [pltpu.SemaphoreType.DMA((max(1, len(windows)),))],
        compiler_params=pltpu.CompilerParams(vmem_limit_bytes=(WINDOW_VMEM if windows else VMEM)),
        cost_estimate=pl.CostEstimate(flops=0, bytes_accessed=0, transcendentals=0),
    )(*arrays)


def pack_body(k, coords, weights, message, points=None):
    rows = message.shape[0] - PAD
    where = coords()
    message[rows : rows + PAD, :] = jnp.zeros((PAD, message.shape[1]), F32)
    message[rows : rows + 3, :] = where[:, k * rows : (k + 1) * rows]
    if points is not None:
        points[...] = jnp.zeros(points.shape, F32)
        points[0:3, :] = where
    message[0:rows, :] = weights()


def flag_of(mask, offset):
    me, count = lax.axis_index("leaf"), lax.axis_size("leaf")
    slot = jnp.where(offset < 0, offset + 2, offset + 1)
    at = me + offset
    return jnp.where((at >= 0) & (at < count), mask[0, slot], 0).astype(F32)


KINDS = ("beside", "across", "passed", "crossed")


def tile(points, message, flag=None):
    rows = message.shape[0] - PAD
    own = points[...].T
    dist = jnp.zeros((own.shape[0], rows), F32)
    for coord in range(3):
        diff = own[:, coord : coord + 1] - message[rows + coord : rows + coord + 1, :]
        dist = dist + diff * diff
    values = message[0:rows, :]
    if flag is not None:
        values = values * flag
    return product(split(jnp.exp(-0.5 * dist)), split(values))


def own_body(points, mask, *refs):
    messages, total, flags = refs[:-2], refs[-2], refs[-1]
    me = lax.axis_index("leaf")
    one, two = 1 - 2 * (me & 1), 2 - 4 * ((me >> 1) & 1)
    flags[...] = jnp.zeros(flags.shape, F32)
    for k, offset in enumerate((one, two, -two, -one)):
        flags[k : k + 1, :] = jnp.full((1, flags.shape[1]), flag_of(mask, offset))
    acc = tile(points, messages[0])
    for message in messages[1:]:
        acc = acc + tile(points, message)
    total[...] = acc


def add_body(kinds, total, points, flags, *rest):
    messages, out = rest[:-1], rest[-1]
    acc = total[...]
    for kind, message in zip(kinds, messages):
        k = KINDS.index(kind)
        acc = acc + tile(points, message, flags[k : k + 1, :])
    out[...] = acc


def start_body(total, points, flags, message, start_high, start_low, near_high, near_low, skeleton):
    k = KINDS.index("crossed")
    near = split(0.5 * (total[...] + tile(points, message, flags[k : k + 1, :])))
    skeleton[...] = product(parts((start_high, start_low)), near)
    put((near_high, near_low), ..., near)


def scale_of(level):
    return 1.0 / math.sqrt(2.0 ** (level + 1))


def halves_by_core(value, mine, other):
    core, half = lax.axis_index("leaf") & 1, mine.shape[0]
    low, high = value[0:half], value[half : 2 * half]
    mine[...] = jnp.where(core == 0, low, high)
    other[...] = jnp.where(core == 0, high, low)


def open_body(up, inverse, start_high, start_low, inverse_high, inverse_low):
    up_parts = split(up().T)
    inverse_parts = split(inverse())
    put((inverse_high, inverse_low), ..., inverse_parts)
    put((start_high, start_low), ..., split(product(up_parts, inverse_parts)))


def fold_body(level, ahead, split_rows, *refs):
    _, down, coupling = refs[0:3]
    refs = refs[3:]
    if ahead:
        up, refs = refs[0], refs[1:]
    down_parts = split(down())
    put(refs[0:2], ..., down_parts)
    step = split(product(down_parts, split(coupling())) * scale_of(level))
    half = step[0].shape[1] // 2
    columns = [(ALL, slice(k * half, (k + 1) * half)) for k in range(2)]
    for k in range(2):
        put(refs[2:4], k, (step[0][columns[k]], step[1][columns[k]]))
    if ahead:
        up_parts = split(up().T)
        put(refs[4:6], ..., up_parts)
        jump = product(up_parts, step)
        if split_rows:
            halves_by_core(jump, refs[6], refs[7])
        else:
            jump = split(jump)
            for k in range(2):
                put(refs[6:8], k, (jump[0][columns[k]], jump[1][columns[k]]))


def fold(level, up_basis, coupling, down_basis, earlier, split_rows):
    points, rank = up_basis.shape[1:]
    half = rank // 2
    ahead = level + 1 < LEVELS
    ups = [Window(up_basis, (level + 1,), (points, rank))] * ahead
    outs = two_parts(points, rank) + two_parts(2, points, half)
    if ahead:
        outs = outs + two_parts(rank, points)
        outs = outs + ([((half, rank), F32)] * 2 if split_rows else two_parts(2, rank, half))
    got = call(
        functools.partial(fold_body, level, ahead, split_rows),
        outs,
        earlier,
        Window(down_basis, (level,), (points, rank)),
        Window(coupling, (level, ALL, slice(rank, 2 * rank)), (rank, rank)),
        *ups,
    )
    return got[0:2], got[2:4], got[4:6], got[6:8]


def settle_first_body(near_high, near_low, skeleton, inverse_high, inverse_low, coupling, down_high, down_low, up_high, up_low, iterate, mine, other):
    weights = split(coupling())
    value = product(parts((inverse_high, inverse_low)), parts((near_high, near_low)))
    middle = product(weights, split(skeleton[...]))
    value = value - product(parts((down_high, down_low)), split(middle * scale_of(0)))
    iterate[...] = value
    halves_by_core(product(parts((up_high, up_low)), split(value)), mine, other)


def settle_body(level, count, ahead, split_rows, *refs):
    base_iterate, old_high, old_low = refs[0:3]
    theirs, refs = refs[3 : 3 + count], refs[3 + count :]
    mine, other, coupling, down_high, down_low = refs[0:5]
    core = lax.axis_index("leaf") & 1
    half = mine.shape[0]
    value = base_iterate[...]
    if count == 1:
        pieces = [(k, theirs[0][k * half : (k + 1) * half, :]) for k in range(2)]
    else:
        pieces = [(core, theirs[0][...]), (1 - core, theirs[1][...])]
    for k, piece in pieces:
        value = value - product(parts((old_high, old_low), k), split(piece))
    low = jnp.where(core == 0, mine[...], other[...])
    high = jnp.where(core == 0, other[...], mine[...])
    middle = product(split(coupling()), split(jnp.concatenate([low, high])))
    value = value - product(parts((down_high, down_low)), split(middle * scale_of(level)))
    if ahead:
        up_high, up_low, iterate = refs[5:8]
        base = product(parts((up_high, up_low)), split(value))
        if split_rows:
            halves_by_core(base, refs[8], refs[9])
        else:
            refs[8][...] = base
    else:
        iterate = refs[5]
    iterate[...] = value


def settle(level, iterate, old, theirs, mine, other, coupling, downs, ups, split_rows):
    points, columns = iterate.shape
    half, rank = mine.shape[0], coupling.shape[2] // 2
    ahead = len(ups) > 0
    outs = [((points, columns), F32)]
    if ahead:
        outs = outs + ([((half, columns), F32)] * 2 if split_rows else [((rank, columns), F32)])
    return call(
        functools.partial(settle_body, level, len(theirs), ahead, split_rows),
        outs,
        iterate,
        *old,
        *theirs,
        mine,
        other,
        Window(coupling, (level, ALL, slice(0, rank)), (rank, rank)),
        *downs,
        *ups,
    )


def join_body(jump_mine, jump_sent, base_mine, base_sent, jump_high, jump_low, base):
    half = base.shape[0]
    for k in range(2):
        at = ALL, slice(k * half, (k + 1) * half)
        put((jump_high, jump_low), k, split(jump_mine[at] + jump_sent[at]))
    base[...] = base_mine[...] + base_sent[...]


def join(jump, base):
    half, rank = jump[0].shape
    columns = base[0].shape[1]
    return call(
        join_body, two_parts(2, half, half) + [((half, columns), F32)], *jump, *base
    )


def sub_body(side, base, factor_high, factor_low, value, out):
    core = lax.axis_index("leaf") & 1
    at = core if side == 0 else 1 - core
    out[...] = base[...] - product(parts((factor_high, factor_low), at), split(value[...]))


def rows_body(turn, base, factor_high, factor_low, value, out):
    core = lax.axis_index("leaf") & 1
    half = out.shape[0]
    rows = pl.ds(pl.multiple_of((1 - core if turn else core) * half, half), half)
    out[...] = base[rows, :] - product(
        parts((factor_high, factor_low), (1 - core, rows)), split(value[...])
    )


def rows_of(turn, base, factor, value):
    rows, columns = base.shape
    return call(functools.partial(rows_body, turn), [((rows // 2, columns), F32)], base, *factor, value)[0]


def sub(side, base, factor, value):
    return call(functools.partial(sub_body, side), [(base.shape, F32)], base, *factor, value)[0]


def sub_whole_body(*refs):
    jump, value, out = refs[-3:]
    acc = refs[0][...]
    for ref in refs[1:-3]:
        acc = acc + ref[...]
    out[...] = acc - product(split(jump[...]), split(value[...]))


def sub_whole(bases, jump, value):
    return call(sub_whole_body, [(bases[0].shape, F32)], *bases, jump, value)[0]


def per_device(coords, weights, near_mask, leaf_inverse, up_basis, coupling, down_basis):
    points, columns = weights.shape
    rank = up_basis.shape[2]
    rows = points // CHUNKS
    me = lax.axis_index("leaf")
    same = (me & 1) == ((me >> 1) & 1)
    bases = up_basis, coupling, down_basis

    def pack(k):
        outs = [((rows + PAD, columns), F32)] + [((8, points), F32)] * (k == 0)
        return call(
            functools.partial(pack_body, k),
            outs,
            Window(coords, (ALL, ALL), (3, points)),
            Window(weights, (slice(k * rows, (k + 1) * rows),), (rows, columns)),
        )

    message, where = pack(0)
    messages = [message, pack(1)[0]]
    across = [exchange(messages[0], 2)]
    far = permute(messages[1], lambda i: i + 4 if i & 2 else i - 4)
    across = across + [exchange(messages[1], 2)]
    beside = [exchange(m, 1) for m in messages]

    total, flags = call(
        own_body,
        [((points, columns), F32), ((8, columns), F32)],
        where,
        near_mask,
        *messages,
    )
    opening = call(
        open_body,
        two_parts(rank, points) + two_parts(points, points),
        Window(up_basis, (0,), (points, rank)),
        Window(leaf_inverse, (ALL,), (points, points)),
    )

    def add(total, **kinds):
        return call(
            functools.partial(add_body, [k for k, v in kinds.items() for _ in v]),
            [((points, columns), F32)],
            total,
            where,
            flags,
            *[m for v in kinds.values() for m in v],
        )[0]

    total = add(total, beside=beside)
    across[0] = after(across[0], total)
    passed = [permute(across[0], lambda i: i - 4 if i & 2 else i + 4)]
    passed = passed + [exchange(far, 2)]
    downs, factor, ups, jump = fold(0, *bases, total, True)
    jump_sent = exchange(jump[1], 1)
    total = add(total, across=across)
    crossed = [exchange(jnp.where(same, across[0], after(passed[0], total, *opening, *factor)), 1)]
    total = add(total, passed=passed[:1])
    far = after(passed[1], total)
    crossed = crossed + [exchange(jnp.where(same, across[1], far), 1)]
    total = add(total, passed=[far], crossed=crossed[:1])
    *near, skeleton = call(
        start_body,
        two_parts(points, columns) + [((rank, columns), F32)],
        total,
        where,
        flags,
        crossed[1],
        *opening[0:2],
    )

    half = rank // 2
    partner = exchange(skeleton, 1)
    iterate, base_mine, base_other = call(
        settle_first_body,
        [((points, columns), F32)] + [((half, columns), F32)] * 2,
        *near,
        skeleton,
        *opening[2:4],
        Window(coupling, (0, ALL, slice(0, rank)), (rank, rank)),
        *downs,
        *ups,
    )
    base = sub_whole((base_mine, exchange(base_other, 1)), jump_sent, skeleton)
    partner = after(partner, base)
    mine = sub_whole((base,), jump[0], partner)
    theirs = [partner]

    for level in range(1, LEVELS):
        ahead, joined = level + 1 < LEVELS, level == 2
        downs, next_factor, ups, jump = fold(level, *bases, mine, joined)
        pending = (*downs, *next_factor, *ups, *jump)
        for even, odd in {1: (), 2: ((2, 2),), 3: ((4, 2), (2, 4))}[level]:
            got = permute(mine, lambda i: i ^ (odd if i & 1 else even))
            mine = mine + after(got, *pending)
            pending = ()
        arriving = exchange(mine, 1 << level)
        other = exchange(mine, 1)
        if joined:
            jump = jump[0], exchange(jump[1], 1)
        iterate, *base = settle(
            level, iterate, factor, theirs, mine, other, coupling, downs, ups, joined
        )
        factor = next_factor
        arriving = after(arriving, iterate, *base)
        theirs = [arriving, exchange(arriving, 1)]
        if joined:
            base_other = after(base[1], arriving)
            *jump, base = join(jump, (base[0], exchange(base_other, 1)))
            mine = sub(1, sub(0, base, jump, theirs[0]), jump, theirs[1])
        elif ahead:
            base = sub(0, base[0], jump, theirs[0])
            mine = rows_of(0, base, jump, theirs[1]) + exchange(
                rows_of(1, base, jump, theirs[1]), 1
            )
    return sub(1, sub(0, iterate, factor, theirs[0]), factor, theirs[1])


def solution(mesh):
    in_specs = (
        P(None, "leaf"),
        P("leaf", None),
        P("leaf", None),
        P("leaf", None),
        P(None, "leaf", None),
        P(None, "leaf", None),
        P(None, "leaf", None),
    )
    return jax.shard_map(
        per_device, mesh=mesh, in_specs=in_specs, out_specs=P("leaf", None), check_vma=False
    )
```

```python
import functools
import math
from typing import Any, NamedTuple

import jax
import jax.numpy as jnp
from jax import lax
from jax.experimental import pallas as pl
from jax.experimental.pallas import tpu as pltpu
from jax.sharding import PartitionSpec as P

LEVELS = 4
CHUNKS = 2
PAD = 8
F32, BF16 = jnp.float32, jnp.bfloat16
VMEM, WINDOW_VMEM = 24 * 2**20, 48 * 2**20
ALL = slice(None)


def permute(x, target):
    count = lax.axis_size("leaf")
    return lax.ppermute(x, "leaf", [(i, target(i) % count) for i in range(count)])


def exchange(x, bit):
    return permute(x, lambda i: i ^ bit)


def after(x, *earlier):
    return lax.optimization_barrier((x, *earlier))[0]


def split(x):
    high = x.astype(BF16)
    return high, (x - high.astype(F32)).astype(BF16)


def product(left, right):
    def dot(a, b):
        return jnp.dot(a, b, preferred_element_type=F32)

    (left_high, left_low), (right_high, right_low) = left, right
    rows, columns = left_high.shape[0], right_high.shape[1]
    count = 2 if columns <= 256 else 1
    got = []
    for k in range(count):
        at = slice(k * rows // count, (k + 1) * rows // count)
        high, low = left_high[at], left_low[at]
        got.append(dot(high, right_high) + (dot(high, right_low) + dot(low, right_high)))
    return jnp.concatenate(got) if count > 1 else got[0]


def parts(refs, index=...):
    return tuple(ref[index] for ref in refs)


def put(refs, index, values):
    for ref, value in zip(refs, values):
        ref[index] = value


def two_parts(*shape):
    return [(shape, BF16)] * 2


class Window(NamedTuple):
    array: Any
    index: tuple
    shape: tuple


class Arriving:
    def __init__(self, copy, ref):
        self.copy, self.ref, self.here = copy, ref, False

    def __call__(self):
        if not self.here:
            self.copy.wait()
            self.here = True
        return self.ref[...]


def call(body, outs, *args):
    windows = [arg for arg in args if isinstance(arg, Window)]
    arrays = [arg.array if isinstance(arg, Window) else arg for arg in args]

    def kernel(*refs):
        ins, rest = list(refs[: len(args)]), refs[len(args) :]
        results, buffers, semaphores = rest[: len(outs)], rest[len(outs) : -1], rest[-1]
        arriving = []
        for k, arg in enumerate(args):
            if isinstance(arg, Window):
                at = len(arriving)
                copy = pltpu.make_async_copy(ins[k].at[arg.index], buffers[at], semaphores.at[at])
                copy.start()
                ins[k] = Arriving(copy, buffers[at])
                arriving.append(ins[k])
        body(*ins, *results)
        for window in arriving:
            if not window.here:
                window.copy.wait()

    def spec(arg):
        if isinstance(arg, Window):
            return pl.BlockSpec(memory_space=pltpu.HBM)
        return pl.BlockSpec(memory_space=pltpu.SMEM if arg.dtype == jnp.int32 else pltpu.VMEM)

    return pl.pallas_call(
        kernel,
        in_specs=[spec(arg) for arg in args],
        out_specs=[pl.BlockSpec(memory_space=pltpu.VMEM) for _ in outs],
        out_shape=[jax.ShapeDtypeStruct(*out) for out in outs],
        scratch_shapes=[pltpu.VMEM(w.shape, w.array.dtype) for w in windows]
        + [pltpu.SemaphoreType.DMA((max(1, len(windows)),))],
        compiler_params=pltpu.CompilerParams(vmem_limit_bytes=(WINDOW_VMEM if windows else VMEM)),
        cost_estimate=pl.CostEstimate(flops=0, bytes_accessed=0, transcendentals=0),
    )(*arrays)


def pack_body(k, coords, weights, message, points=None):
    rows = message.shape[0] - PAD
    where = coords()
    message[rows : rows + PAD, :] = jnp.zeros((PAD, message.shape[1]), F32)
    message[rows : rows + 3, :] = where[:, k * rows : (k + 1) * rows]
    if points is not None:
        points[...] = jnp.zeros(points.shape, F32)
        points[0:3, :] = where
    message[0:rows, :] = weights()


def flag_of(mask, offset):
    me, count = lax.axis_index("leaf"), lax.axis_size("leaf")
    slot = jnp.where(offset < 0, offset + 2, offset + 1)
    at = me + offset
    return jnp.where((at >= 0) & (at < count), mask[0, slot], 0).astype(F32)


KINDS = ("beside", "across", "passed", "crossed")


def tile(points, message, flag=None):
    rows = message.shape[0] - PAD
    own = points[...].T
    dist = jnp.zeros((own.shape[0], rows), F32)
    for coord in range(3):
        diff = own[:, coord : coord + 1] - message[rows + coord : rows + coord + 1, :]
        dist = dist + diff * diff
    values = message[0:rows, :]
    if flag is not None:
        values = values * flag
    return product(split(jnp.exp(-0.5 * dist)), split(values))


def own_body(points, mask, *refs):
    messages, total, flags = refs[:-2], refs[-2], refs[-1]
    me = lax.axis_index("leaf")
    one, two = 1 - 2 * (me & 1), 2 - 4 * ((me >> 1) & 1)
    flags[...] = jnp.zeros(flags.shape, F32)
    for k, offset in enumerate((one, two, -two, -one)):
        flags[k : k + 1, :] = jnp.full((1, flags.shape[1]), flag_of(mask, offset))
    acc = tile(points, messages[0])
    for message in messages[1:]:
        acc = acc + tile(points, message)
    total[...] = acc


def add_body(kinds, total, points, flags, *rest):
    messages, out = rest[:-1], rest[-1]
    acc = total[...]
    for kind, message in zip(kinds, messages):
        k = KINDS.index(kind)
        acc = acc + tile(points, message, flags[k : k + 1, :])
    out[...] = acc


def start_body(total, points, flags, message, start_high, start_low, near_high, near_low, skeleton):
    k = KINDS.index("crossed")
    near = split(0.5 * (total[...] + tile(points, message, flags[k : k + 1, :])))
    skeleton[...] = product(parts((start_high, start_low)), near)
    put((near_high, near_low), ..., near)


def scale_of(level):
    return 1.0 / math.sqrt(2.0 ** (level + 1))


def halves_by_core(value, mine, other):
    core, half = lax.axis_index("leaf") & 1, mine.shape[0]
    low, high = value[0:half], value[half : 2 * half]
    mine[...] = jnp.where(core == 0, low, high)
    other[...] = jnp.where(core == 0, high, low)


def open_body(up, inverse, coupling, down, up_next, *outs):
    up_parts = split(up().T)
    inverse_parts = split(inverse())
    put(outs[0:2], ..., split(product(up_parts, inverse_parts)))
    put(outs[2:4], ..., inverse_parts)
    put(outs[4:6], ..., split(coupling()))
    put(outs[6:8], ..., split(down()))
    put(outs[8:10], ..., split(up_next().T))


def first_body(near_high, near_low, skeleton, inverse_high, inverse_low, high, low, iterate, middle):
    rank = skeleton.shape[0]
    middle[...] = product((high[:, 0:rank], low[:, 0:rank]), split(skeleton[...]))
    iterate[...] = product(parts((inverse_high, inverse_low)), parts((near_high, near_low)))


def second_body(iterate, middle, partner, high, low, down_high, down_low, up_high, up_low, out, mine, other):
    rank = partner.shape[0]
    factor = high[:, rank : 2 * rank], low[:, rank : 2 * rank]
    correction = (middle[...] + product(factor, split(partner[...]))) * scale_of(0)
    value = iterate[...] - product(parts((down_high, down_low)), split(correction))
    halves_by_core(product(parts((up_high, up_low)), split(value)), mine, other)
    out[...] = value


def fold_body(level, ahead, split_rows, *refs):
    _, down, coupling = refs[0:3]
    refs = refs[3:]
    if ahead:
        up, refs = refs[0], refs[1:]
    down_parts = split(down())
    put(refs[0:2], ..., down_parts)
    step = split(product(down_parts, split(coupling())) * scale_of(level))
    half = step[0].shape[1] // 2
    columns = [(ALL, slice(k * half, (k + 1) * half)) for k in range(2)]
    for k in range(2):
        put(refs[2:4], k, (step[0][columns[k]], step[1][columns[k]]))
    if ahead:
        up_parts = split(up().T)
        put(refs[4:6], ..., up_parts)
        jump = product(up_parts, step)
        if split_rows:
            halves_by_core(jump, refs[6], refs[7])
        else:
            jump = split(jump)
            for k in range(2):
                put(refs[6:8], k, (jump[0][columns[k]], jump[1][columns[k]]))


def fold(level, up_basis, coupling, down_basis, earlier, split_rows):
    points, rank = up_basis.shape[1:]
    half = rank // 2
    ahead = level + 1 < LEVELS
    ups = [Window(up_basis, (level + 1,), (points, rank))] * ahead
    outs = two_parts(points, rank) + two_parts(2, points, half)
    if ahead:
        outs = outs + two_parts(rank, points)
        outs = outs + ([((half, rank), F32)] * 2 if split_rows else two_parts(2, rank, half))
    got = call(
        functools.partial(fold_body, level, ahead, split_rows),
        outs,
        earlier,
        Window(down_basis, (level,), (points, rank)),
        Window(coupling, (level, ALL, slice(rank, 2 * rank)), (rank, rank)),
        *ups,
    )
    return got[0:2], got[2:4], got[4:6], got[6:8]


def settle_body(level, count, ahead, split_rows, *refs):
    base_iterate, refs = refs[0], refs[1:]
    if count:
        old, theirs, refs = refs[0:2], refs[2 : 2 + count], refs[2 + count :]
    mine, other, coupling, down_high, down_low = refs[0:5]
    core = lax.axis_index("leaf") & 1
    half = mine.shape[0]
    value = base_iterate[...]
    for k in range(count):
        at = core if k == 0 else 1 - core
        value = value - product(parts(old, at), split(theirs[k][...]))
    low = jnp.where(core == 0, mine[...], other[...])
    high = jnp.where(core == 0, other[...], mine[...])
    middle = product(split(coupling()), split(jnp.concatenate([low, high])))
    value = value - product(parts((down_high, down_low)), split(middle * scale_of(level)))
    if ahead:
        up_high, up_low, iterate = refs[5:8]
        base = product(parts((up_high, up_low)), split(value))
        if split_rows:
            halves_by_core(base, refs[8], refs[9])
        else:
            refs[8][...] = base
    else:
        iterate = refs[5]
    iterate[...] = value


def settle(level, iterate, old, theirs, mine, other, coupling, downs, ups, split_rows):
    points, columns = iterate.shape
    half, rank = mine.shape[0], coupling.shape[2] // 2
    ahead = len(ups) > 0
    outs = [((points, columns), F32)]
    if ahead:
        outs = outs + ([((half, columns), F32)] * 2 if split_rows else [((rank, columns), F32)])
    return call(
        functools.partial(settle_body, level, len(theirs), ahead, split_rows),
        outs,
        iterate,
        *old,
        *theirs,
        mine,
        other,
        Window(coupling, (level, ALL, slice(0, rank)), (rank, rank)),
        *downs,
        *ups,
    )


def join_body(jump_mine, jump_sent, base_mine, base_sent, jump_high, jump_low, base):
    half = base.shape[0]
    for k in range(2):
        at = ALL, slice(k * half, (k + 1) * half)
        put((jump_high, jump_low), k, split(jump_mine[at] + jump_sent[at]))
    base[...] = base_mine[...] + base_sent[...]


def join(jump, base):
    half, rank = jump[0].shape
    columns = base[0].shape[1]
    return call(
        join_body, two_parts(2, half, half) + [((half, columns), F32)], *jump, *base
    )


def sub_body(side, base, factor_high, factor_low, value, out):
    core = lax.axis_index("leaf") & 1
    at = core if side == 0 else 1 - core
    out[...] = base[...] - product(parts((factor_high, factor_low), at), split(value[...]))


def rows_body(turn, base, factor_high, factor_low, value, out):
    core = lax.axis_index("leaf") & 1
    half = out.shape[0]
    rows = pl.ds(pl.multiple_of((1 - core if turn else core) * half, half), half)
    out[...] = base[rows, :] - product(
        parts((factor_high, factor_low), (1 - core, rows)), split(value[...])
    )


def rows_of(turn, base, factor, value):
    rows, columns = base.shape
    return call(functools.partial(rows_body, turn), [((rows // 2, columns), F32)], base, *factor, value)[0]


def sub(side, base, factor, value):
    return call(functools.partial(sub_body, side), [(base.shape, F32)], base, *factor, value)[0]


def per_device(coords, weights, near_mask, leaf_inverse, up_basis, coupling, down_basis):
    points, columns = weights.shape
    rank = up_basis.shape[2]
    rows = points // CHUNKS
    me = lax.axis_index("leaf")
    same = (me & 1) == ((me >> 1) & 1)
    bases = up_basis, coupling, down_basis

    def pack(k):
        outs = [((rows + PAD, columns), F32)] + [((8, points), F32)] * (k == 0)
        return call(
            functools.partial(pack_body, k),
            outs,
            Window(coords, (ALL, ALL), (3, points)),
            Window(weights, (slice(k * rows, (k + 1) * rows),), (rows, columns)),
        )

    message, where = pack(0)
    messages = [message, pack(1)[0]]
    across = [exchange(messages[0], 2)]
    far = permute(messages[1], lambda i: i + 4 if i & 2 else i - 4)
    across = across + [exchange(messages[1], 2)]
    beside = [exchange(m, 1) for m in messages]

    total, flags = call(
        own_body,
        [((points, columns), F32), ((8, columns), F32)],
        where,
        near_mask,
        *messages,
    )
    opening = call(
        open_body,
        two_parts(rank, points) + two_parts(points, points) + two_parts(rank, 2 * rank)
        + two_parts(points, rank) + two_parts(rank, points),
        Window(up_basis, (0,), (points, rank)),
        Window(leaf_inverse, (ALL,), (points, points)),
        Window(coupling, (0,), (rank, 2 * rank)),
        Window(down_basis, (0,), (points, rank)),
        Window(up_basis, (1,), (points, rank)),
    )

    def add(total, **kinds):
        return call(
            functools.partial(add_body, [k for k, v in kinds.items() for _ in v]),
            [((points, columns), F32)],
            total,
            where,
            flags,
            *[m for v in kinds.values() for m in v],
        )[0]

    total = add(total, beside=beside)
    across[0] = after(across[0], total)
    passed = [permute(across[0], lambda i: i - 4 if i & 2 else i + 4)]
    passed = passed + [exchange(far, 2)]
    total = add(total, across=across)
    crossed = [exchange(jnp.where(same, across[0], after(passed[0], total, *opening)), 1)]
    total = add(total, passed=passed[:1])
    far = after(passed[1], total)
    crossed = crossed + [exchange(jnp.where(same, across[1], far), 1)]
    total = add(total, passed=[far], crossed=crossed[:1])
    *near, skeleton = call(
        start_body,
        two_parts(points, columns) + [((rank, columns), F32)],
        total,
        where,
        flags,
        crossed[1],
        *opening[0:2],
    )

    half = rank // 2
    partner = exchange(skeleton, 1)
    iterate, middle = call(
        first_body,
        [((points, columns), F32), ((rank, columns), F32)],
        *near,
        skeleton,
        *opening[2:6],
    )
    partner = after(partner, iterate, middle)
    iterate, base_mine, base_other = call(
        second_body,
        [((points, columns), F32)] + [((half, columns), F32)] * 2,
        iterate,
        middle,
        partner,
        *opening[4:10],
    )
    mine = base_mine + exchange(base_other, 1)
    factor, theirs = (), ()

    for level in range(1, LEVELS):
        ahead, joined = level + 1 < LEVELS, level == 2
        downs, next_factor, ups, jump = fold(level, *bases, mine, joined)
        pending = (*downs, *next_factor, *ups, *jump)
        for even, odd in {1: (), 2: ((2, 2),), 3: ((4, 2), (2, 4))}[level]:
            got = permute(mine, lambda i: i ^ (odd if i & 1 else even))
            mine = mine + after(got, *pending)
            pending = ()
        arriving = exchange(mine, 1 << level)
        other = exchange(mine, 1)
        if joined:
            jump = jump[0], exchange(jump[1], 1)
        iterate, *base = settle(
            level, iterate, factor, theirs, mine, other, coupling, downs, ups, joined
        )
        factor = next_factor
        arriving = after(arriving, iterate, *base)
        theirs = [arriving, exchange(arriving, 1)]
        if joined:
            base_other = after(base[1], arriving)
            *jump, base = join(jump, (base[0], exchange(base_other, 1)))
            mine = sub(1, sub(0, base, jump, theirs[0]), jump, theirs[1])
        elif ahead:
            base = sub(0, base[0], jump, theirs[0])
            mine = rows_of(0, base, jump, theirs[1]) + exchange(
                rows_of(1, base, jump, theirs[1]), 1
            )
    return sub(1, sub(0, iterate, factor, theirs[0]), factor, theirs[1])


def solution(mesh):
    in_specs = (
        P(None, "leaf"),
        P("leaf", None),
        P("leaf", None),
        P("leaf", None),
        P(None, "leaf", None),
        P(None, "leaf", None),
        P(None, "leaf", None),
    )
    return jax.shard_map(
        per_device, mesh=mesh, in_specs=in_specs, out_specs=P("leaf", None), check_vma=False
    )
```

```python
import functools
import math
from typing import Any, NamedTuple

import jax
import jax.numpy as jnp
from jax import lax
from jax.experimental import pallas as pl
from jax.experimental.pallas import tpu as pltpu
from jax.sharding import PartitionSpec as P

LEVELS = 4
CHUNKS = 2
PAD = 8
F32, BF16 = jnp.float32, jnp.bfloat16
VMEM, WINDOW_VMEM = 24 * 2**20, 48 * 2**20
ALL = slice(None)


def permute(x, target):
    count = lax.axis_size("leaf")
    pairs = [(i, target(i)) for i in range(count)]
    return lax.ppermute(x, "leaf", [(i, j) for i, j in pairs if 0 <= j < count])


def exchange(x, bit):
    return permute(x, lambda i: i ^ bit)


def after(x, *earlier):
    return lax.optimization_barrier((x, *earlier))[0]


def split(x):
    high = x.astype(BF16)
    return high, (x - high.astype(F32)).astype(BF16)


def product(left, right):
    def dot(a, b):
        return jnp.dot(a, b, preferred_element_type=F32)

    (left_high, left_low), (right_high, right_low) = left, right
    rows, columns = left_high.shape[0], right_high.shape[1]
    count = 2 if columns <= 256 else 1
    got = []
    for k in range(count):
        at = slice(k * rows // count, (k + 1) * rows // count)
        high, low = left_high[at], left_low[at]
        got.append(dot(high, right_high) + (dot(high, right_low) + dot(low, right_high)))
    return jnp.concatenate(got) if count > 1 else got[0]


def parts(refs, index=...):
    return tuple(ref[index] for ref in refs)


def put(refs, index, values):
    for ref, value in zip(refs, values):
        ref[index] = value


def two_parts(*shape):
    return [(shape, BF16)] * 2


class Window(NamedTuple):
    array: Any
    index: tuple
    shape: tuple


class Arriving:
    def __init__(self, copy, ref):
        self.copy, self.ref, self.here = copy, ref, False

    def __call__(self):
        if not self.here:
            self.copy.wait()
            self.here = True
        return self.ref[...]


def call(body, outs, *args):
    windows = [arg for arg in args if isinstance(arg, Window)]
    arrays = [arg.array if isinstance(arg, Window) else arg for arg in args]

    def kernel(*refs):
        ins, rest = list(refs[: len(args)]), refs[len(args) :]
        results, buffers, semaphores = rest[: len(outs)], rest[len(outs) : -1], rest[-1]
        arriving = []
        for k, arg in enumerate(args):
            if isinstance(arg, Window):
                at = len(arriving)
                copy = pltpu.make_async_copy(ins[k].at[arg.index], buffers[at], semaphores.at[at])
                copy.start()
                ins[k] = Arriving(copy, buffers[at])
                arriving.append(ins[k])
        body(*ins, *results)
        for window in arriving:
            if not window.here:
                window.copy.wait()

    def spec(arg):
        if isinstance(arg, Window):
            return pl.BlockSpec(memory_space=pltpu.HBM)
        return pl.BlockSpec(memory_space=pltpu.SMEM if arg.dtype == jnp.int32 else pltpu.VMEM)

    return pl.pallas_call(
        kernel,
        in_specs=[spec(arg) for arg in args],
        out_specs=[pl.BlockSpec(memory_space=pltpu.VMEM) for _ in outs],
        out_shape=[jax.ShapeDtypeStruct(*out) for out in outs],
        scratch_shapes=[pltpu.VMEM(w.shape, w.array.dtype) for w in windows]
        + [pltpu.SemaphoreType.DMA((max(1, len(windows)),))],
        compiler_params=pltpu.CompilerParams(vmem_limit_bytes=(WINDOW_VMEM if windows else VMEM)),
        cost_estimate=pl.CostEstimate(flops=0, bytes_accessed=0, transcendentals=0),
    )(*arrays)


def pack_body(k, coords, weights, message, points=None):
    rows = message.shape[0] - PAD
    where = coords()
    message[rows : rows + PAD, :] = jnp.zeros((PAD, message.shape[1]), F32)
    message[rows : rows + 3, :] = where[:, k * rows : (k + 1) * rows]
    if points is not None:
        points[...] = jnp.zeros(points.shape, F32)
        points[0:3, :] = where
    message[0:rows, :] = weights()


def flag_of(mask, offset):
    me, count = lax.axis_index("leaf"), lax.axis_size("leaf")
    slot = jnp.where(offset < 0, offset + 2, offset + 1)
    at = me + offset
    return jnp.where((at >= 0) & (at < count), mask[0, slot], 0).astype(F32)


KINDS = ("beside", "across", "passed", "crossed")


def tile(points, message, flag=None):
    rows = message.shape[0] - PAD
    own = points[...].T
    dist = jnp.zeros((own.shape[0], rows), F32)
    for coord in range(3):
        diff = own[:, coord : coord + 1] - message[rows + coord : rows + coord + 1, :]
        dist = dist + diff * diff
    values = message[0:rows, :]
    if flag is not None:
        values = values * flag
    return product(split(jnp.exp(-0.5 * dist)), split(values))


def own_body(points, mask, *refs):
    messages, total, flags = refs[:-2], refs[-2], refs[-1]
    me = lax.axis_index("leaf")
    one, two = 1 - 2 * (me & 1), 2 - 4 * ((me >> 1) & 1)
    flags[...] = jnp.zeros(flags.shape, F32)
    for k, offset in enumerate((one, two, -two, -one)):
        flags[k : k + 1, :] = jnp.full((1, flags.shape[1]), flag_of(mask, offset))
    acc = tile(points, messages[0])
    for message in messages[1:]:
        acc = acc + tile(points, message)
    total[...] = acc


def add_body(kinds, total, points, flags, *rest):
    messages, out = rest[:-1], rest[-1]
    acc = total[...]
    for kind, message in zip(kinds, messages):
        k = KINDS.index(kind)
        acc = acc + tile(points, message, flags[k : k + 1, :])
    out[...] = acc


def start_body(total, points, flags, message, start_high, start_low, near_high, near_low, skeleton):
    k = KINDS.index("crossed")
    near = split(0.5 * (total[...] + tile(points, message, flags[k : k + 1, :])))
    skeleton[...] = product(parts((start_high, start_low)), near)
    put((near_high, near_low), ..., near)


def scale_of(level):
    return 1.0 / math.sqrt(2.0 ** (level + 1))


def halves_by_core(value, mine, other):
    core, half = lax.axis_index("leaf") & 1, mine.shape[0]
    low, high = value[0:half], value[half : 2 * half]
    mine[...] = jnp.where(core == 0, low, high)
    other[...] = jnp.where(core == 0, high, low)


def open_body(up, inverse, coupling, down, up_next, *outs):
    up_parts = split(up().T)
    inverse_parts = split(inverse())
    put(outs[0:2], ..., split(product(up_parts, inverse_parts)))
    put(outs[2:4], ..., inverse_parts)
    put(outs[4:6], ..., split(coupling()))
    put(outs[6:8], ..., split(down()))
    put(outs[8:10], ..., split(up_next().T))


def first_body(near_high, near_low, skeleton, inverse_high, inverse_low, high, low, iterate, middle):
    rank = skeleton.shape[0]
    middle[...] = product((high[:, 0:rank], low[:, 0:rank]), split(skeleton[...]))
    iterate[...] = product(parts((inverse_high, inverse_low)), parts((near_high, near_low)))


def second_body(iterate, middle, partner, high, low, down_high, down_low, up_high, up_low, out, mine, other):
    rank = partner.shape[0]
    factor = high[:, rank : 2 * rank], low[:, rank : 2 * rank]
    correction = (middle[...] + product(factor, split(partner[...]))) * scale_of(0)
    value = iterate[...] - product(parts((down_high, down_low)), split(correction))
    halves_by_core(product(parts((up_high, up_low)), split(value)), mine, other)
    out[...] = value


def fold_body(level, ahead, split_rows, *refs):
    _, down, coupling = refs[0:3]
    refs = refs[3:]
    if ahead:
        up, refs = refs[0], refs[1:]
    down_parts = split(down())
    put(refs[0:2], ..., down_parts)
    step = split(product(down_parts, split(coupling())) * scale_of(level))
    half = step[0].shape[1] // 2
    columns = [(ALL, slice(k * half, (k + 1) * half)) for k in range(2)]
    for k in range(2):
        put(refs[2:4], k, (step[0][columns[k]], step[1][columns[k]]))
    if ahead:
        up_parts = split(up().T)
        put(refs[4:6], ..., up_parts)
        jump = product(up_parts, step)
        if split_rows:
            halves_by_core(jump, refs[6], refs[7])
        else:
            jump = split(jump)
            for k in range(2):
                put(refs[6:8], k, (jump[0][columns[k]], jump[1][columns[k]]))


def fold(level, up_basis, coupling, down_basis, earlier, split_rows):
    points, rank = up_basis.shape[1:]
    half = rank // 2
    ahead = level + 1 < LEVELS
    ups = [Window(up_basis, (level + 1,), (points, rank))] * ahead
    outs = two_parts(points, rank) + two_parts(2, points, half)
    if ahead:
        outs = outs + two_parts(rank, points)
        outs = outs + ([((half, rank), F32)] * 2 if split_rows else two_parts(2, rank, half))
    got = call(
        functools.partial(fold_body, level, ahead, split_rows),
        outs,
        earlier,
        Window(down_basis, (level,), (points, rank)),
        Window(coupling, (level, ALL, slice(rank, 2 * rank)), (rank, rank)),
        *ups,
    )
    return got[0:2], got[2:4], got[4:6], got[6:8]


def settle_body(level, count, ahead, split_rows, *refs):
    base_iterate, refs = refs[0], refs[1:]
    if count:
        old, theirs, refs = refs[0:2], refs[2 : 2 + count], refs[2 + count :]
    mine, other, coupling, down_high, down_low = refs[0:5]
    core = lax.axis_index("leaf") & 1
    half = mine.shape[0]
    value = base_iterate[...]
    for k in range(count):
        at = core if k == 0 else 1 - core
        value = value - product(parts(old, at), split(theirs[k][...]))
    low = jnp.where(core == 0, mine[...], other[...])
    high = jnp.where(core == 0, other[...], mine[...])
    middle = product(split(coupling()), split(jnp.concatenate([low, high])))
    value = value - product(parts((down_high, down_low)), split(middle * scale_of(level)))
    if ahead:
        up_high, up_low, iterate = refs[5:8]
        base = product(parts((up_high, up_low)), split(value))
        if split_rows:
            halves_by_core(base, refs[8], refs[9])
        else:
            refs[8][...] = base
    else:
        iterate = refs[5]
    iterate[...] = value


def settle(level, iterate, old, theirs, mine, other, coupling, downs, ups, split_rows):
    points, columns = iterate.shape
    half, rank = mine.shape[0], coupling.shape[2] // 2
    ahead = len(ups) > 0
    outs = [((points, columns), F32)]
    if ahead:
        outs = outs + ([((half, columns), F32)] * 2 if split_rows else [((rank, columns), F32)])
    return call(
        functools.partial(settle_body, level, len(theirs), ahead, split_rows),
        outs,
        iterate,
        *old,
        *theirs,
        mine,
        other,
        Window(coupling, (level, ALL, slice(0, rank)), (rank, rank)),
        *downs,
        *ups,
    )


def join_body(jump_mine, jump_sent, base_mine, base_sent, jump_high, jump_low, base):
    half = base.shape[0]
    for k in range(2):
        at = ALL, slice(k * half, (k + 1) * half)
        put((jump_high, jump_low), k, split(jump_mine[at] + jump_sent[at]))
    base[...] = base_mine[...] + base_sent[...]


def join(jump, base):
    half, rank = jump[0].shape
    columns = base[0].shape[1]
    return call(
        join_body, two_parts(2, half, half) + [((half, columns), F32)], *jump, *base
    )


def sub_body(side, base, factor_high, factor_low, value, out):
    core = lax.axis_index("leaf") & 1
    at = core if side == 0 else 1 - core
    out[...] = base[...] - product(parts((factor_high, factor_low), at), split(value[...]))


def rows_body(turn, base, factor_high, factor_low, value, out):
    core = lax.axis_index("leaf") & 1
    half = out.shape[0]
    rows = pl.ds(pl.multiple_of((1 - core if turn else core) * half, half), half)
    out[...] = base[rows, :] - product(
        parts((factor_high, factor_low), (1 - core, rows)), split(value[...])
    )


def rows_of(turn, base, factor, value):
    rows, columns = base.shape
    return call(functools.partial(rows_body, turn), [((rows // 2, columns), F32)], base, *factor, value)[0]


def sub(side, base, factor, value):
    return call(functools.partial(sub_body, side), [(base.shape, F32)], base, *factor, value)[0]


def per_device(coords, weights, near_mask, leaf_inverse, up_basis, coupling, down_basis):
    points, columns = weights.shape
    rank = up_basis.shape[2]
    rows = points // CHUNKS
    me = lax.axis_index("leaf")
    same = (me & 1) == ((me >> 1) & 1)
    bases = up_basis, coupling, down_basis

    def pack(k):
        outs = [((rows + PAD, columns), F32)] + [((8, points), F32)] * (k == 0)
        return call(
            functools.partial(pack_body, k),
            outs,
            Window(coords, (ALL, ALL), (3, points)),
            Window(weights, (slice(k * rows, (k + 1) * rows),), (rows, columns)),
        )

    message, where = pack(0)
    messages = [message, pack(1)[0]]
    across = [exchange(messages[0], 2)]
    far = permute(messages[1], lambda i: i + 4 if i & 2 else i - 4)
    across = across + [exchange(messages[1], 2)]

    total, flags = call(
        own_body,
        [((points, columns), F32), ((8, columns), F32)],
        where,
        near_mask,
        *messages,
    )
    opening = call(
        open_body,
        two_parts(rank, points) + two_parts(points, points) + two_parts(rank, 2 * rank)
        + two_parts(points, rank) + two_parts(rank, points),
        Window(up_basis, (0,), (points, rank)),
        Window(leaf_inverse, (ALL,), (points, points)),
        Window(coupling, (0,), (rank, 2 * rank)),
        Window(down_basis, (0,), (points, rank)),
        Window(up_basis, (1,), (points, rank)),
    )

    def add(total, **kinds):
        return call(
            functools.partial(add_body, [k for k, v in kinds.items() for _ in v]),
            [((points, columns), F32)],
            total,
            where,
            flags,
            *[m for v in kinds.values() for m in v],
        )[0]

    beside = [exchange(m, 1) for m in after(messages, total)]
    across[0] = after(across[0], total)
    passed = [permute(across[0], lambda i: i - 4 if i & 2 else i + 4)]
    passed = passed + [exchange(far, 2)]
    total = add(total, beside=beside, across=across)
    crossed = [exchange(jnp.where(same, across[0], after(passed[0], total, *opening)), 1)]
    total = add(total, passed=passed[:1])
    far = after(passed[1], total)
    crossed = crossed + [exchange(jnp.where(same, across[1], far), 1)]
    total = add(total, passed=[far], crossed=crossed[:1])
    *near, skeleton = call(
        start_body,
        two_parts(points, columns) + [((rank, columns), F32)],
        total,
        where,
        flags,
        crossed[1],
        *opening[0:2],
    )

    half = rank // 2
    partner = exchange(skeleton, 1)
    iterate, middle = call(
        first_body,
        [((points, columns), F32), ((rank, columns), F32)],
        *near,
        skeleton,
        *opening[2:6],
    )
    partner = after(partner, iterate, middle)
    iterate, base_mine, base_other = call(
        second_body,
        [((points, columns), F32)] + [((half, columns), F32)] * 2,
        iterate,
        middle,
        partner,
        *opening[4:10],
    )
    mine = base_mine + exchange(base_other, 1)
    factor, theirs = (), ()

    for level in range(1, LEVELS):
        ahead, joined = level + 1 < LEVELS, level == 2
        downs, next_factor, ups, jump = fold(level, *bases, mine, joined)
        pending = (*downs, *next_factor, *ups, *jump)
        for even, odd in {1: (), 2: ((2, 2),), 3: ((4, 2), (2, 4))}[level]:
            got = permute(mine, lambda i: i ^ (odd if i & 1 else even))
            mine = mine + after(got, *pending)
            pending = ()
        arriving = exchange(mine, 1 << level)
        other = jnp.concatenate([exchange(m, 1) for m in jnp.split(mine, 2)])
        if joined:
            jump = jump[0], exchange(jump[1], 1)
        iterate, *base = settle(
            level, iterate, factor, theirs, mine, other, coupling, downs, ups, joined
        )
        factor = next_factor
        arriving = after(arriving, iterate, *base)
        theirs = [arriving, exchange(arriving, 1)]
        if joined:
            base_other = after(base[1], arriving)
            *jump, base = join(jump, (base[0], exchange(base_other, 1)))
            mine = sub(1, sub(0, base, jump, theirs[0]), jump, theirs[1])
        elif ahead:
            base = sub(0, base[0], jump, theirs[0])
            mine = rows_of(0, base, jump, theirs[1]) + exchange(
                rows_of(1, base, jump, theirs[1]), 1
            )
    return sub(1, sub(0, iterate, factor, theirs[0]), factor, theirs[1])


def solution(mesh):
    in_specs = (
        P(None, "leaf"),
        P("leaf", None),
        P("leaf", None),
        P("leaf", None),
        P(None, "leaf", None),
        P(None, "leaf", None),
        P(None, "leaf", None),
    )
    return jax.shard_map(
        per_device, mesh=mesh, in_specs=in_specs, out_specs=P("leaf", None), check_vma=False
    )
```

```python
import functools
import math
from typing import Any, NamedTuple

import jax
import jax.numpy as jnp
from jax import lax
from jax.experimental import pallas as pl
from jax.experimental.pallas import tpu as pltpu
from jax.sharding import PartitionSpec as P

LEVELS = 4
CHUNKS = 2
PAD = 8
F32, BF16 = jnp.float32, jnp.bfloat16
VMEM, WINDOW_VMEM = 24 * 2**20, 48 * 2**20
ALL = slice(None)
PIECES = {1: 1, 2: 1, 3: 2}


def permute(x, target):
    count = lax.axis_size("leaf")
    pairs = [(i, target(i)) for i in range(count)]
    return lax.ppermute(x, "leaf", [(i, j) for i, j in pairs if 0 <= j < count])


def exchange(x, bit):
    return permute(x, lambda i: i ^ bit)


def after(x, *earlier):
    return lax.optimization_barrier((x, *earlier))[0]


def split(x):
    high = x.astype(BF16)
    return high, (x - high.astype(F32)).astype(BF16)


def product(left, right):
    def dot(a, b):
        return jnp.dot(a, b, preferred_element_type=F32)

    (left_high, left_low), (right_high, right_low) = left, right
    rows, columns = left_high.shape[0], right_high.shape[1]
    count = 2 if columns <= 256 else 1
    got = []
    for k in range(count):
        at = slice(k * rows // count, (k + 1) * rows // count)
        high, low = left_high[at], left_low[at]
        got.append(dot(high, right_high) + (dot(high, right_low) + dot(low, right_high)))
    return jnp.concatenate(got) if count > 1 else got[0]


def parts(refs, index=...):
    return tuple(ref[index] for ref in refs)


def put(refs, index, values):
    for ref, value in zip(refs, values):
        ref[index] = value


def joined_rows(refs):
    return jnp.concatenate([ref[...] for ref in refs]) if len(refs) > 1 else refs[0][...]


def cut(x, count):
    return jnp.split(x, count)


def two_parts(*shape):
    return [(shape, BF16)] * 2


class Window(NamedTuple):
    array: Any
    index: tuple
    shape: tuple


class Arriving:
    def __init__(self, copy, ref):
        self.copy, self.ref, self.here = copy, ref, False

    def __call__(self):
        if not self.here:
            self.copy.wait()
            self.here = True
        return self.ref[...]


def call(body, outs, *args):
    windows = [arg for arg in args if isinstance(arg, Window)]
    arrays = [arg.array if isinstance(arg, Window) else arg for arg in args]

    def kernel(*refs):
        ins, rest = list(refs[: len(args)]), refs[len(args) :]
        results, buffers, semaphores = rest[: len(outs)], rest[len(outs) : -1], rest[-1]
        arriving = []
        for k, arg in enumerate(args):
            if isinstance(arg, Window):
                at = len(arriving)
                copy = pltpu.make_async_copy(ins[k].at[arg.index], buffers[at], semaphores.at[at])
                copy.start()
                ins[k] = Arriving(copy, buffers[at])
                arriving.append(ins[k])
        body(*ins, *results)
        for window in arriving:
            if not window.here:
                window.copy.wait()

    def spec(arg):
        if isinstance(arg, Window):
            return pl.BlockSpec(memory_space=pltpu.HBM)
        return pl.BlockSpec(memory_space=pltpu.SMEM if arg.dtype == jnp.int32 else pltpu.VMEM)

    return pl.pallas_call(
        kernel,
        in_specs=[spec(arg) for arg in args],
        out_specs=[pl.BlockSpec(memory_space=pltpu.VMEM) for _ in outs],
        out_shape=[jax.ShapeDtypeStruct(*out) for out in outs],
        scratch_shapes=[pltpu.VMEM(w.shape, w.array.dtype) for w in windows]
        + [pltpu.SemaphoreType.DMA((max(1, len(windows)),))],
        compiler_params=pltpu.CompilerParams(vmem_limit_bytes=(WINDOW_VMEM if windows else VMEM)),
        cost_estimate=pl.CostEstimate(flops=0, bytes_accessed=0, transcendentals=0),
    )(*arrays)


def pack_body(k, points, weights, message):
    rows = message.shape[0] - PAD
    message[rows : rows + PAD, :] = points[:, k * rows : (k + 1) * rows]
    message[0:rows, :] = weights()


def flag_of(mask, offset):
    me, count = lax.axis_index("leaf"), lax.axis_size("leaf")
    slot = jnp.where(offset < 0, offset + 2, offset + 1)
    at = me + offset
    return jnp.where((at >= 0) & (at < count), mask[0, slot], 0).astype(F32)


KINDS = ("beside", "across", "passed", "crossed")


def tile(points, message, flag=None):
    rows = message.shape[0] - PAD
    own = points[...].T
    dist = jnp.zeros((own.shape[0], rows), F32)
    for coord in range(3):
        diff = own[:, coord : coord + 1] - message[rows + coord : rows + coord + 1, :]
        dist = dist + diff * diff
    values = message[0:rows, :]
    if flag is not None:
        values = values * flag
    return product(split(jnp.exp(-0.5 * dist)), split(values))


def own_body(points, mask, *refs):
    messages, total, flags = refs[:-2], refs[-2], refs[-1]
    me = lax.axis_index("leaf")
    one, two = 1 - 2 * (me & 1), 2 - 4 * ((me >> 1) & 1)
    flags[...] = jnp.zeros(flags.shape, F32)
    for k, offset in enumerate((one, two, -two, -one)):
        flags[k : k + 1, :] = jnp.full((1, flags.shape[1]), flag_of(mask, offset))
    acc = tile(points, messages[0])
    for message in messages[1:]:
        acc = acc + tile(points, message)
    total[...] = acc


def add_body(kinds, total, points, flags, *rest):
    messages, out = rest[:-1], rest[-1]
    acc = total[...]
    for kind, message in zip(kinds, messages):
        k = KINDS.index(kind)
        acc = acc + tile(points, message, flags[k : k + 1, :])
    out[...] = acc


def start_body(total, points, flags, *refs):
    start_high, start_low, near_high, near_low, skeleton = refs[-5:]
    k, message = KINDS.index("crossed"), joined_rows(refs[:-5])
    near = split(0.5 * (total[...] + tile(points, message, flags[k : k + 1, :])))
    skeleton[...] = product(parts((start_high, start_low)), near)
    put((near_high, near_low), ..., near)


def scale_of(level):
    return 1.0 / math.sqrt(2.0 ** (level + 1))


def halves_by_core(value, mine, other):
    core, half = lax.axis_index("leaf") & 1, mine.shape[0]
    low, high = value[0:half], value[half : 2 * half]
    mine[...] = jnp.where(core == 0, low, high)
    other[...] = jnp.where(core == 0, high, low)


def open_body(up, inverse, coupling, down, up_next, *outs):
    up_parts = split(up().T)
    inverse_parts = split(inverse())
    put(outs[0:2], ..., split(product(up_parts, inverse_parts)))
    put(outs[2:4], ..., inverse_parts)
    put(outs[4:6], ..., split(coupling()))
    put(outs[6:8], ..., split(down()))
    put(outs[8:10], ..., split(up_next().T))


def first_body(near_high, near_low, skeleton, inverse_high, inverse_low, high, low, iterate, middle):
    rank = skeleton.shape[0]
    middle[...] = product((high[:, 0:rank], low[:, 0:rank]), split(skeleton[...]))
    iterate[...] = product(parts((inverse_high, inverse_low)), parts((near_high, near_low)))


def second_body(iterate, middle, partner, high, low, down_high, down_low, up_high, up_low, out, mine, other):
    rank = partner.shape[0]
    factor = high[:, rank : 2 * rank], low[:, rank : 2 * rank]
    correction = (middle[...] + product(factor, split(partner[...]))) * scale_of(0)
    value = iterate[...] - product(parts((down_high, down_low)), split(correction))
    halves_by_core(product(parts((up_high, up_low)), split(value)), mine, other)
    out[...] = value


def fold_body(level, ahead, split_rows, *refs):
    _, down, coupling = refs[0:3]
    refs = refs[3:]
    if ahead:
        up, refs = refs[0], refs[1:]
    if level > 1:
        own, refs = refs[0], refs[1:]
        put(refs[-2:], ..., split(own()))
    down_parts = split(down())
    put(refs[0:2], ..., down_parts)
    step = split(product(down_parts, split(coupling())) * scale_of(level))
    half = step[0].shape[1] // 2
    columns = [(ALL, slice(k * half, (k + 1) * half)) for k in range(2)]
    for k in range(2):
        put(refs[2:4], k, (step[0][columns[k]], step[1][columns[k]]))
    if ahead:
        up_parts = split(up().T)
        put(refs[4:6], ..., up_parts)
        jump = product(up_parts, step)
        if split_rows:
            halves_by_core(jump, refs[6], refs[7])
        else:
            jump = split(jump)
            for k in range(2):
                put(refs[6:8], k, (jump[0][columns[k]], jump[1][columns[k]]))


def fold(level, up_basis, coupling, down_basis, earlier, split_rows):
    points, rank = up_basis.shape[1:]
    half = rank // 2
    ahead = level + 1 < LEVELS
    ups = [Window(up_basis, (level + 1,), (points, rank))] * ahead
    outs = two_parts(points, rank) + two_parts(2, points, half)
    if ahead:
        outs = outs + two_parts(rank, points)
        outs = outs + ([((half, rank), F32)] * 2 if split_rows else two_parts(2, rank, half))
    owns = [Window(coupling, (level, ALL, slice(0, rank)), (rank, rank))] * (level > 1)
    outs = outs + two_parts(rank, rank) * len(owns)
    got = call(
        functools.partial(fold_body, level, ahead, split_rows),
        outs,
        earlier,
        Window(down_basis, (level,), (points, rank)),
        Window(coupling, (level, ALL, slice(rank, 2 * rank)), (rank, rank)),
        *ups,
        *owns,
    )
    owned = got[-2:] if owns else ()
    got = got[:-2] if owns else got
    return got[0:2], got[2:4], got[4:6], got[6:8], owned


def complete_body(count, iterate, factor_high, factor_low, *refs):
    core = lax.axis_index("leaf") & 1
    value = iterate[...]
    for k, at in enumerate((core, 1 - core)):
        theirs = joined_rows(refs[k * count : (k + 1) * count])
        value = value - product(parts((factor_high, factor_low), at), split(theirs))
    refs[-1][...] = value


def complete(iterate, factor, theirs):
    pieces = [piece for half_of in theirs for piece in half_of]
    return call(
        functools.partial(complete_body, len(theirs[0])), [(iterate.shape, F32)], iterate, *factor, *pieces
    )[0]


def settle_body(level, counts, ahead, split_rows, *refs):
    base_iterate, refs = refs[0], refs[1:]
    core = lax.axis_index("leaf") & 1
    value = base_iterate[...]
    if counts[0]:
        old, refs = refs[0:2], refs[2:]
        for at in (core, 1 - core):
            theirs, refs = refs[: counts[0]], refs[counts[0] :]
            value = value - product(parts(old, at), split(joined_rows(theirs)))
    mine, refs = joined_rows(refs[: counts[1]]), refs[counts[1] :]
    other, refs = joined_rows(refs[: counts[2]]), refs[counts[2] :]
    if level > 1:
        own, refs = parts(refs[0:2]), refs[1:]
    else:
        own = split(refs[0]())
    down_high, down_low = refs[1:3]
    low = jnp.where(core == 0, mine, other)
    high = jnp.where(core == 0, other, mine)
    middle = product(own, split(jnp.concatenate([low, high])))
    value = value - product(parts((down_high, down_low)), split(middle * scale_of(level)))
    if ahead:
        up_high, up_low, iterate = refs[3:6]
        base = product(parts((up_high, up_low)), split(value))
        if split_rows:
            halves_by_core(base, refs[6], refs[7])
        else:
            refs[6][...] = base
    else:
        iterate = refs[3]
    iterate[...] = value


def settle(level, iterate, old, theirs, mine, other, coupling, owned, downs, ups, split_rows):
    points, columns = iterate.shape
    rank = coupling.shape[2] // 2
    half = rank // 2
    ahead = len(ups) > 0
    outs = [((points, columns), F32)]
    if ahead:
        outs = outs + ([((half, columns), F32)] * 2 if split_rows else [((rank, columns), F32)])
    counts = len(theirs[0]) if theirs else 0, len(mine), len(other)
    return call(
        functools.partial(settle_body, level, counts, ahead, split_rows),
        outs,
        iterate,
        *old,
        *[piece for half_of in theirs for piece in half_of],
        *mine,
        *other,
        *(owned or [Window(coupling, (level, ALL, slice(0, rank)), (rank, rank))]),
        *downs,
        *ups,
    )


def join_body(mine, sent, high, low):
    half = mine.shape[0]
    for k in range(2):
        at = ALL, slice(k * half, (k + 1) * half)
        put((high, low), k, split(mine[at] + sent[at]))


def join(mine, sent):
    half, rank = mine.shape
    return call(join_body, two_parts(2, half, half), mine, sent)


def add_sub_body(base, sent, factor_high, factor_low, *refs):
    at = 1 - (lax.axis_index("leaf") & 1)
    change = product(parts((factor_high, factor_low), at), split(joined_rows(refs[:-1])))
    refs[-1][...] = (base[...] + sent[...]) - change


def add_sub(base, sent, factor, value):
    return call(add_sub_body, [(base.shape, F32)], base, sent, *factor, *value)[0]


def sub_body(side, base, factor_high, factor_low, *refs):
    core = lax.axis_index("leaf") & 1
    at = core if side == 0 else 1 - core
    value = joined_rows(refs[:-1])
    refs[-1][...] = base[...] - product(parts((factor_high, factor_low), at), split(value))


def rows_body(turn, base, factor_high, factor_low, *refs):
    core = lax.axis_index("leaf") & 1
    out = refs[-1]
    half = out.shape[0]
    rows = pl.ds(pl.multiple_of((1 - core if turn else core) * half, half), half)
    out[...] = base[rows, :] - product(
        parts((factor_high, factor_low), (1 - core, rows)), split(joined_rows(refs[:-1]))
    )


def rows_of(turn, base, factor, value):
    rows, columns = base.shape
    return call(functools.partial(rows_body, turn), [((rows // 2, columns), F32)], base, *factor, *value)[0]


def sub(side, base, factor, value):
    return call(functools.partial(sub_body, side), [(base.shape, F32)], base, *factor, *value)[0]


def finish_body(base, factor_high, factor_low, *refs):
    out, buffer, semaphores = refs[-3:]
    at = 1 - (lax.axis_index("leaf") & 1)
    value = split(joined_rows(refs[:-3]))
    half = buffer.shape[0] // 2
    copies = []
    for k in range(2):
        rows = pl.ds(k * half, half)
        change = product(parts((factor_high, factor_low), (at, rows)), value)
        buffer[rows, :] = base[rows, :] - change
        copies.append(pltpu.make_async_copy(buffer.at[rows], out.at[rows], semaphores.at[k]))
        copies[k].start()
    for copy in copies:
        copy.wait()


def finish(base, factor, value):
    args = (base, *factor, *value)
    return pl.pallas_call(
        finish_body,
        in_specs=[pl.BlockSpec(memory_space=pltpu.VMEM) for _ in args],
        out_specs=pl.BlockSpec(memory_space=pltpu.HBM),
        out_shape=jax.ShapeDtypeStruct(base.shape, F32),
        scratch_shapes=[pltpu.VMEM(base.shape, F32), pltpu.SemaphoreType.DMA((2,))],
        compiler_params=pltpu.CompilerParams(vmem_limit_bytes=VMEM),
        cost_estimate=pl.CostEstimate(flops=0, bytes_accessed=0, transcendentals=0),
    )(*args)


def per_device(coords, weights, near_mask, leaf_inverse, up_basis, coupling, down_basis):
    points, columns = weights.shape
    rank = up_basis.shape[2]
    rows = points // CHUNKS
    me = lax.axis_index("leaf")
    same = (me & 1) == ((me >> 1) & 1)
    bases = up_basis, coupling, down_basis

    where = jnp.pad(coords, ((0, PAD - 3), (0, 0)))

    def pack(k):
        return call(
            functools.partial(pack_body, k),
            [((rows + PAD, columns), F32)],
            where,
            Window(weights, (slice(k * rows, (k + 1) * rows),), (rows, columns)),
        )

    messages = [pack(k)[0] for k in range(CHUNKS)]
    across = [exchange(messages[0], 2)]
    far = permute(messages[1], lambda i: i + 4 if i & 2 else i - 4)
    across = across + [exchange(messages[1], 2)]

    total, flags = call(
        own_body,
        [((points, columns), F32), ((8, columns), F32)],
        where,
        near_mask,
        *messages,
    )
    opening = call(
        open_body,
        two_parts(rank, points) + two_parts(points, points) + two_parts(rank, 2 * rank)
        + two_parts(points, rank) + two_parts(rank, points),
        Window(up_basis, (0,), (points, rank)),
        Window(leaf_inverse, (ALL,), (points, points)),
        Window(coupling, (0,), (rank, 2 * rank)),
        Window(down_basis, (0,), (points, rank)),
        Window(up_basis, (1,), (points, rank)),
    )

    def add(total, **kinds):
        return call(
            functools.partial(add_body, [k for k, v in kinds.items() for _ in v]),
            [((points, columns), F32)],
            total,
            where,
            flags,
            *[m for v in kinds.values() for m in v],
        )[0]

    beside = [exchange(m, 1) for m in after(messages, total)]
    across[0] = after(across[0], total)
    passed = [permute(across[0], lambda i: i - 4 if i & 2 else i + 4)]
    passed = passed + [exchange(far, 2)]
    total = add(total, beside=beside, across=across)
    crossed = [exchange(jnp.where(same, across[0], after(passed[0], total, *opening)), 1)]
    total = add(total, passed=passed[:1])
    far = after(passed[1], total)
    near_cut = (rows + PAD) // 16 * 8
    last = [
        exchange(jnp.where(same, across[1][at], far[at]), 1)
        for at in (slice(0, near_cut), slice(near_cut, rows + PAD))
    ]
    total = add(add(total, passed=[far]), crossed=crossed[:1])
    *near, skeleton = call(
        start_body,
        two_parts(points, columns) + [((rank, columns), F32)],
        total,
        where,
        flags,
        *last,
        *opening[0:2],
    )

    half = rank // 2
    partner = exchange(skeleton, 1)
    iterate, middle = call(
        first_body,
        [((points, columns), F32), ((rank, columns), F32)],
        *near,
        skeleton,
        *opening[2:6],
    )
    partner = after(partner, iterate, middle)
    iterate, base_mine, base_other = call(
        second_body,
        [((points, columns), F32)] + [((half, columns), F32)] * 2,
        iterate,
        middle,
        partner,
        *opening[4:10],
    )
    mine = base_mine + exchange(base_other, 1)
    factor, theirs = (), ()

    for level in range(1, LEVELS):
        ahead, joined = level + 1 < LEVELS, level == 2
        downs, next_factor, ups, jump, owned = fold(level, *bases, mine, joined)
        pending = (*downs, *next_factor, *ups, *jump, *owned)
        if theirs:
            iterate = complete(after(iterate, *next_factor), factor, theirs)
            pending, factor, theirs = (*pending, iterate), (), ()
        mine = cut(mine, PIECES[level])
        for even, odd in {1: (), 2: ((2, 2),), 3: ((4, 2), (2, 4))}[level]:
            got = [permute(m, lambda i: i ^ (odd if i & 1 else even)) for m in mine]
            mine = [m + after(g, *pending) for m, g in zip(mine, got)]
            pending = ()
        arriving = [exchange(m, 1 << level) for m in mine]
        other = [exchange(c, 1) for m in mine for c in cut(m, 2)]
        if joined:
            jump = join(jump[0], exchange(jump[1], 1))
            pending = tuple(jump)
        iterate, *base = settle(
            level, iterate, factor, theirs, mine, other, coupling, owned, downs, ups, joined
        )
        factor = next_factor
        arriving = [after(a, iterate, *base, *pending) for a in arriving]
        theirs = arriving, [exchange(a, 1) for a in arriving]
        if joined:
            base_other = after(base[1], arriving[-1])
            sent = exchange(base_other, 1)
            mine = add_sub(sub(0, base[0], jump, theirs[0]), sent, jump, theirs[1])
        elif ahead:
            base = sub(0, base[0], jump, theirs[0])
            mine = rows_of(0, base, jump, theirs[1]) + exchange(
                rows_of(1, base, jump, theirs[1]), 1
            )
    return finish(sub(0, iterate, factor, theirs[0]), factor, theirs[1])


def solution(mesh):
    in_specs = (
        P(None, "leaf"),
        P("leaf", None),
        P("leaf", None),
        P("leaf", None),
        P(None, "leaf", None),
        P(None, "leaf", None),
        P(None, "leaf", None),
    )
    return jax.shard_map(
        per_device, mesh=mesh, in_specs=in_specs, out_specs=P("leaf", None), check_vma=False
    )
```

```python
import functools
import math
from typing import Any, NamedTuple

import jax
import jax.numpy as jnp
from jax import lax
from jax.experimental import pallas as pl
from jax.experimental.pallas import tpu as pltpu
from jax.sharding import PartitionSpec as P

LEVELS = 4
CHUNKS = 2
PAD = 8
F32, BF16 = jnp.float32, jnp.bfloat16
VMEM, WINDOW_VMEM = 24 * 2**20, 48 * 2**20
ALL = slice(None)
PIECES = {1: 1, 2: 1, 3: 2}


def permute(x, target):
    count = lax.axis_size("leaf")
    pairs = [(i, target(i)) for i in range(count)]
    return lax.ppermute(x, "leaf", [(i, j) for i, j in pairs if 0 <= j < count])


def exchange(x, bit):
    return permute(x, lambda i: i ^ bit)


def after(x, *earlier):
    return lax.optimization_barrier((x, *earlier))[0]


def split(x):
    high = x.astype(BF16)
    return high, (x - high.astype(F32)).astype(BF16)


def product(left, right):
    def dot(a, b):
        return jnp.dot(a, b, preferred_element_type=F32)

    (left_high, left_low), (right_high, right_low) = left, right
    rows, columns = left_high.shape[0], right_high.shape[1]
    count = 2 if columns <= 256 else 1
    got = []
    for k in range(count):
        at = slice(k * rows // count, (k + 1) * rows // count)
        high, low = left_high[at], left_low[at]
        got.append(dot(high, right_high) + (dot(high, right_low) + dot(low, right_high)))
    return jnp.concatenate(got) if count > 1 else got[0]


def parts(refs, index=...):
    return tuple(ref[index] for ref in refs)


def put(refs, index, values):
    for ref, value in zip(refs, values):
        ref[index] = value


def joined_rows(refs):
    return jnp.concatenate([ref[...] for ref in refs]) if len(refs) > 1 else refs[0][...]


def cut(x, count):
    return jnp.split(x, count)


def two_parts(*shape):
    return [(shape, BF16)] * 2


class Window(NamedTuple):
    array: Any
    index: tuple
    shape: tuple


class Arriving:
    def __init__(self, copy, ref):
        self.copy, self.ref, self.here = copy, ref, False

    def __call__(self):
        if not self.here:
            self.copy.wait()
            self.here = True
        return self.ref[...]


def call(body, outs, *args):
    windows = [arg for arg in args if isinstance(arg, Window)]
    arrays = [arg.array if isinstance(arg, Window) else arg for arg in args]

    def kernel(*refs):
        ins, rest = list(refs[: len(args)]), refs[len(args) :]
        results, buffers, semaphores = rest[: len(outs)], rest[len(outs) : -1], rest[-1]
        arriving = []
        for k, arg in enumerate(args):
            if isinstance(arg, Window):
                at = len(arriving)
                copy = pltpu.make_async_copy(ins[k].at[arg.index], buffers[at], semaphores.at[at])
                copy.start()
                ins[k] = Arriving(copy, buffers[at])
                arriving.append(ins[k])
        body(*ins, *results)
        for window in arriving:
            if not window.here:
                window.copy.wait()

    def spec(arg):
        if isinstance(arg, Window):
            return pl.BlockSpec(memory_space=pltpu.HBM)
        return pl.BlockSpec(memory_space=pltpu.SMEM if arg.dtype == jnp.int32 else pltpu.VMEM)

    return pl.pallas_call(
        kernel,
        in_specs=[spec(arg) for arg in args],
        out_specs=[pl.BlockSpec(memory_space=pltpu.VMEM) for _ in outs],
        out_shape=[jax.ShapeDtypeStruct(*out) for out in outs],
        scratch_shapes=[pltpu.VMEM(w.shape, w.array.dtype) for w in windows]
        + [pltpu.SemaphoreType.DMA((max(1, len(windows)),))],
        compiler_params=pltpu.CompilerParams(vmem_limit_bytes=(WINDOW_VMEM if windows else VMEM)),
        cost_estimate=pl.CostEstimate(flops=0, bytes_accessed=0, transcendentals=0),
    )(*arrays)


def pack_body(k, points, weights, message):
    rows = message.shape[0] - PAD
    message[rows : rows + PAD, :] = points[:, k * rows : (k + 1) * rows]
    message[0:rows, :] = weights()


def flag_of(mask, offset):
    me, count = lax.axis_index("leaf"), lax.axis_size("leaf")
    slot = jnp.where(offset < 0, offset + 2, offset + 1)
    at = me + offset
    return jnp.where((at >= 0) & (at < count), mask[0, slot], 0).astype(F32)


KINDS = ("beside", "across", "passed", "crossed")


def tile(points, message, flag=None):
    rows = message.shape[0] - PAD
    own = points[...].T
    dist = jnp.zeros((own.shape[0], rows), F32)
    for coord in range(3):
        diff = own[:, coord : coord + 1] - message[rows + coord : rows + coord + 1, :]
        dist = dist + diff * diff
    values = message[0:rows, :]
    if flag is not None:
        values = values * flag
    return product(split(jnp.exp(-0.5 * dist)), split(values))


def own_body(points, mask, *refs):
    messages, total, flags = refs[:-2], refs[-2], refs[-1]
    me = lax.axis_index("leaf")
    one, two = 1 - 2 * (me & 1), 2 - 4 * ((me >> 1) & 1)
    flags[...] = jnp.zeros(flags.shape, F32)
    for k, offset in enumerate((one, two, -two, -one)):
        flags[k : k + 1, :] = jnp.full((1, flags.shape[1]), flag_of(mask, offset))
    acc = tile(points, messages[0])
    for message in messages[1:]:
        acc = acc + tile(points, message)
    total[...] = acc


def add_body(kinds, total, points, flags, *rest):
    messages, out = rest[:-1], rest[-1]
    acc = total[...]
    for kind, message in zip(kinds, messages):
        k = KINDS.index(kind)
        acc = acc + tile(points, message, flags[k : k + 1, :])
    out[...] = acc


def start_body(total, points, flags, *refs):
    start_high, start_low, near_high, near_low, skeleton = refs[-5:]
    k, message = KINDS.index("crossed"), joined_rows(refs[:-5])
    near = split(0.5 * (total[...] + tile(points, message, flags[k : k + 1, :])))
    skeleton[...] = product(parts((start_high, start_low)), near)
    put((near_high, near_low), ..., near)


def scale_of(level):
    return 1.0 / math.sqrt(2.0 ** (level + 1))


def halves_by_core(value, mine, other):
    core, half = lax.axis_index("leaf") & 1, mine.shape[0]
    low, high = value[0:half], value[half : 2 * half]
    mine[...] = jnp.where(core == 0, low, high)
    other[...] = jnp.where(core == 0, high, low)


def open_body(up, inverse, coupling, down, up_next, *outs):
    up_parts = split(up().T)
    inverse_parts = split(inverse())
    put(outs[0:2], ..., split(product(up_parts, inverse_parts)))
    put(outs[2:4], ..., inverse_parts)
    put(outs[4:6], ..., split(coupling()))
    put(outs[6:8], ..., split(down()))
    put(outs[8:10], ..., split(up_next().T))


def first_body(near_high, near_low, skeleton, inverse_high, inverse_low, high, low, iterate, middle):
    rank = skeleton.shape[0]
    middle[...] = product((high[:, 0:rank], low[:, 0:rank]), split(skeleton[...]))
    iterate[...] = product(parts((inverse_high, inverse_low)), parts((near_high, near_low)))


def second_body(iterate, middle, partner, high, low, down_high, down_low, up_high, up_low, out, mine, other):
    rank = partner.shape[0]
    factor = high[:, rank : 2 * rank], low[:, rank : 2 * rank]
    correction = (middle[...] + product(factor, split(partner[...]))) * scale_of(0)
    value = iterate[...] - product(parts((down_high, down_low)), split(correction))
    halves_by_core(product(parts((up_high, up_low)), split(value)), mine, other)
    out[...] = value


def fold_body(level, ahead, split_rows, *refs):
    _, down, coupling = refs[0:3]
    refs = refs[3:]
    if ahead:
        up, refs = refs[0], refs[1:]
    if level > 1:
        own, refs = refs[0], refs[1:]
        put(refs[-2:], ..., split(own()))
    down_parts = split(down())
    put(refs[0:2], ..., down_parts)
    step = split(product(down_parts, split(coupling())) * scale_of(level))
    half = step[0].shape[1] // 2
    columns = [(ALL, slice(k * half, (k + 1) * half)) for k in range(2)]
    for k in range(2):
        put(refs[2:4], k, (step[0][columns[k]], step[1][columns[k]]))
    if ahead:
        up_parts = split(up().T)
        put(refs[4:6], ..., up_parts)
        jump = product(up_parts, step)
        if split_rows:
            halves_by_core(jump, refs[6], refs[7])
        else:
            jump = split(jump)
            for k in range(2):
                put(refs[6:8], k, (jump[0][columns[k]], jump[1][columns[k]]))


def fold(level, up_basis, coupling, down_basis, earlier, split_rows):
    points, rank = up_basis.shape[1:]
    half = rank // 2
    ahead = level + 1 < LEVELS
    ups = [Window(up_basis, (level + 1,), (points, rank))] * ahead
    outs = two_parts(points, rank) + two_parts(2, points, half)
    if ahead:
        outs = outs + two_parts(rank, points)
        outs = outs + ([((half, rank), F32)] * 2 if split_rows else two_parts(2, rank, half))
    owns = [Window(coupling, (level, ALL, slice(0, rank)), (rank, rank))] * (level > 1)
    outs = outs + two_parts(rank, rank) * len(owns)
    got = call(
        functools.partial(fold_body, level, ahead, split_rows),
        outs,
        earlier,
        Window(down_basis, (level,), (points, rank)),
        Window(coupling, (level, ALL, slice(rank, 2 * rank)), (rank, rank)),
        *ups,
        *owns,
    )
    owned = got[-2:] if owns else ()
    got = got[:-2] if owns else got
    return got[0:2], got[2:4], got[4:6], got[6:8], owned


def complete_body(count, iterate, factor_high, factor_low, *refs):
    core = lax.axis_index("leaf") & 1
    value = iterate[...]
    for k, at in enumerate((core, 1 - core)):
        theirs = joined_rows(refs[k * count : (k + 1) * count])
        value = value - product(parts((factor_high, factor_low), at), split(theirs))
    refs[-1][...] = value


def complete(iterate, factor, theirs):
    pieces = [piece for half_of in theirs for piece in half_of]
    return call(
        functools.partial(complete_body, len(theirs[0])), [(iterate.shape, F32)], iterate, *factor, *pieces
    )[0]


def settle_body(level, counts, ahead, split_rows, *refs):
    base_iterate, refs = refs[0], refs[1:]
    core = lax.axis_index("leaf") & 1
    value = base_iterate[...]
    if counts[0]:
        old, refs = refs[0:2], refs[2:]
        for at in (core, 1 - core):
            theirs, refs = refs[: counts[0]], refs[counts[0] :]
            value = value - product(parts(old, at), split(joined_rows(theirs)))
    mine, refs = joined_rows(refs[: counts[1]]), refs[counts[1] :]
    other, refs = joined_rows(refs[: counts[2]]), refs[counts[2] :]
    if level > 1:
        own, refs = parts(refs[0:2]), refs[1:]
    else:
        own = split(refs[0]())
    down_high, down_low = refs[1:3]
    low = jnp.where(core == 0, mine, other)
    high = jnp.where(core == 0, other, mine)
    middle = product(own, split(jnp.concatenate([low, high])))
    value = value - product(parts((down_high, down_low)), split(middle * scale_of(level)))
    if ahead:
        up_high, up_low, iterate = refs[3:6]
        base = product(parts((up_high, up_low)), split(value))
        if split_rows:
            halves_by_core(base, refs[6], refs[7])
        else:
            refs[6][...] = base
    else:
        iterate = refs[3]
    iterate[...] = value


def settle(level, iterate, old, theirs, mine, other, coupling, owned, downs, ups, split_rows):
    points, columns = iterate.shape
    rank = coupling.shape[2] // 2
    half = rank // 2
    ahead = len(ups) > 0
    outs = [((points, columns), F32)]
    if ahead:
        outs = outs + ([((half, columns), F32)] * 2 if split_rows else [((rank, columns), F32)])
    counts = len(theirs[0]) if theirs else 0, len(mine), len(other)
    return call(
        functools.partial(settle_body, level, counts, ahead, split_rows),
        outs,
        iterate,
        *old,
        *[piece for half_of in theirs for piece in half_of],
        *mine,
        *other,
        *(owned or [Window(coupling, (level, ALL, slice(0, rank)), (rank, rank))]),
        *downs,
        *ups,
    )


def join_body(mine, sent, high, low):
    half = mine.shape[0]
    for k in range(2):
        at = ALL, slice(k * half, (k + 1) * half)
        put((high, low), k, split(mine[at] + sent[at]))


def join(mine, sent):
    half, rank = mine.shape
    return call(join_body, two_parts(2, half, half), mine, sent)


def add_sub_body(base, sent, factor_high, factor_low, *refs):
    at = 1 - (lax.axis_index("leaf") & 1)
    change = product(parts((factor_high, factor_low), at), split(joined_rows(refs[:-1])))
    refs[-1][...] = (base[...] + sent[...]) - change


def add_sub(base, sent, factor, value):
    return call(add_sub_body, [(base.shape, F32)], base, sent, *factor, *value)[0]


def sub_body(side, base, factor_high, factor_low, *refs):
    core = lax.axis_index("leaf") & 1
    at = core if side == 0 else 1 - core
    value = joined_rows(refs[:-1])
    refs[-1][...] = base[...] - product(parts((factor_high, factor_low), at), split(value))


def rows_body(turn, base, factor_high, factor_low, *refs):
    core = lax.axis_index("leaf") & 1
    out = refs[-1]
    half = out.shape[0]
    rows = pl.ds(pl.multiple_of((1 - core if turn else core) * half, half), half)
    out[...] = base[rows, :] - product(
        parts((factor_high, factor_low), (1 - core, rows)), split(joined_rows(refs[:-1]))
    )


def rows_of(turn, base, factor, value):
    rows, columns = base.shape
    return call(functools.partial(rows_body, turn), [((rows // 2, columns), F32)], base, *factor, *value)[0]


def sub(side, base, factor, value):
    return call(functools.partial(sub_body, side), [(base.shape, F32)], base, *factor, *value)[0]


def finish_body(base, factor_high, factor_low, *refs):
    out, buffer, semaphores = refs[-3:]
    at = 1 - (lax.axis_index("leaf") & 1)
    value = split(joined_rows(refs[:-3]))
    half = buffer.shape[0] // 2
    copies = []
    for k in range(2):
        rows = pl.ds(k * half, half)
        change = product(parts((factor_high, factor_low), (at, rows)), value)
        buffer[rows, :] = base[rows, :] - change
        copies.append(pltpu.make_async_copy(buffer.at[rows], out.at[rows], semaphores.at[k]))
        copies[k].start()
    for copy in copies:
        copy.wait()


def finish(base, factor, value):
    args = (base, *factor, *value)
    return pl.pallas_call(
        finish_body,
        in_specs=[pl.BlockSpec(memory_space=pltpu.VMEM) for _ in args],
        out_specs=pl.BlockSpec(memory_space=pltpu.HBM),
        out_shape=jax.ShapeDtypeStruct(base.shape, F32),
        scratch_shapes=[pltpu.VMEM(base.shape, F32), pltpu.SemaphoreType.DMA((2,))],
        compiler_params=pltpu.CompilerParams(vmem_limit_bytes=VMEM),
        cost_estimate=pl.CostEstimate(flops=0, bytes_accessed=0, transcendentals=0),
    )(*args)


def per_device(coords, weights, near_mask, leaf_inverse, up_basis, coupling, down_basis):
    points, columns = weights.shape
    rank = up_basis.shape[2]
    rows = points // CHUNKS
    me = lax.axis_index("leaf")
    same = (me & 1) == ((me >> 1) & 1)
    bases = up_basis, coupling, down_basis

    where = jnp.pad(coords, ((0, PAD - 3), (0, 0)))

    def pack(k):
        return call(
            functools.partial(pack_body, k),
            [((rows + PAD, columns), F32)],
            where,
            Window(weights, (slice(k * rows, (k + 1) * rows),), (rows, columns)),
        )

    messages = [pack(k)[0] for k in range(CHUNKS)]
    across = [exchange(messages[0], 2)]
    far = permute(messages[1], lambda i: i + 4 if i & 2 else i - 4)
    across = across + [exchange(messages[1], 2)]

    total, flags = call(
        own_body,
        [((points, columns), F32), ((8, columns), F32)],
        where,
        near_mask,
        *messages,
    )
    opening = call(
        open_body,
        two_parts(rank, points) + two_parts(points, points) + two_parts(rank, 2 * rank)
        + two_parts(points, rank) + two_parts(rank, points),
        Window(up_basis, (0,), (points, rank)),
        Window(leaf_inverse, (ALL,), (points, points)),
        Window(coupling, (0,), (rank, 2 * rank)),
        Window(down_basis, (0,), (points, rank)),
        Window(up_basis, (1,), (points, rank)),
    )

    def add(total, **kinds):
        return call(
            functools.partial(add_body, [k for k, v in kinds.items() for _ in v]),
            [((points, columns), F32)],
            total,
            where,
            flags,
            *[m for v in kinds.values() for m in v],
        )[0]

    beside = [exchange(m, 1) for m in after(messages, total)]
    across[0] = after(across[0], total)
    passed = [permute(across[0], lambda i: i - 4 if i & 2 else i + 4)]
    passed = passed + [exchange(far, 2)]
    total = add(total, beside=beside, across=across)
    crossed = [exchange(jnp.where(same, across[0], after(passed[0], total, *opening)), 1)]
    total = add(total, passed=passed[:1])
    far = after(passed[1], total)
    near_cut = (rows + PAD) // 16 * 8
    last = [
        exchange(jnp.where(same, across[1][at], far[at]), 1)
        for at in (slice(0, near_cut), slice(near_cut, rows + PAD))
    ]
    total = add(total, passed=[far], crossed=crossed[:1])
    *near, skeleton = call(
        start_body,
        two_parts(points, columns) + [((rank, columns), F32)],
        total,
        where,
        flags,
        *last,
        *opening[0:2],
    )

    half = rank // 2
    partner = exchange(skeleton, 1)
    iterate, middle = call(
        first_body,
        [((points, columns), F32), ((rank, columns), F32)],
        *near,
        skeleton,
        *opening[2:6],
    )
    partner = after(partner, iterate, middle)
    iterate, base_mine, base_other = call(
        second_body,
        [((points, columns), F32)] + [((half, columns), F32)] * 2,
        iterate,
        middle,
        partner,
        *opening[4:10],
    )
    mine = base_mine + exchange(base_other, 1)
    factor, theirs = (), ()

    for level in range(1, LEVELS):
        ahead, joined = level + 1 < LEVELS, level == 2
        downs, next_factor, ups, jump, owned = fold(level, *bases, mine, joined)
        pending = (*downs, *next_factor, *ups, *jump, *owned)
        if theirs:
            iterate = complete(after(iterate, *next_factor), factor, theirs)
            pending, factor, theirs = (*pending, iterate), (), ()
        mine = cut(mine, PIECES[level])
        for even, odd in {1: (), 2: ((2, 2),), 3: ((4, 2), (2, 4))}[level]:
            got = [permute(m, lambda i: i ^ (odd if i & 1 else even)) for m in mine]
            mine = [m + after(g, *pending) for m, g in zip(mine, got)]
            pending = ()
        arriving = [exchange(m, 1 << level) for m in mine]
        other = [exchange(c, 1) for m in mine for c in cut(m, 2)]
        if joined:
            jump = join(jump[0], exchange(jump[1], 1))
            pending = tuple(jump)
        iterate, *base = settle(
            level, iterate, factor, theirs, mine, other, coupling, owned, downs, ups, joined
        )
        factor = next_factor
        arriving = [after(a, iterate, *base, *pending) for a in arriving]
        theirs = arriving, [exchange(a, 1) for a in arriving]
        if joined:
            base_other = after(base[1], arriving[-1])
            sent = exchange(base_other, 1)
            mine = add_sub(sub(0, base[0], jump, theirs[0]), sent, jump, theirs[1])
        elif ahead:
            base = sub(0, base[0], jump, theirs[0])
            mine = rows_of(0, base, jump, theirs[1]) + exchange(
                rows_of(1, base, jump, theirs[1]), 1
            )
    return finish(sub(0, iterate, factor, theirs[0]), factor, theirs[1])


def solution(mesh):
    in_specs = (
        P(None, "leaf"),
        P("leaf", None),
        P("leaf", None),
        P("leaf", None),
        P(None, "leaf", None),
        P(None, "leaf", None),
        P(None, "leaf", None),
    )
    return jax.shard_map(
        per_device, mesh=mesh, in_specs=in_specs, out_specs=P("leaf", None), check_vma=False
    )
```
